128 devices in a mesh: gx: 16 (over y, x_hi, core), gy: 8 (over z, x_lo).
Axes of the slice: x: 4 (x_hi: 2, x_lo: 2; x = x_hi * 2 + x_lo), y: 4, z: 4, core: 2. Of those that a mesh axis runs over, the one named last changes fastest.
Arguments:
- slab_tokens: bfloat16 [32, 16, 32, 512], P('gx', None, 'gy'), may hold values from -6 to 6
- cotangent: bfloat16 [32, 16, 32, 512], P('gx', 'gy'), may hold values from -6 to 6
- w_qkv: bfloat16 [1536, 512], replicated, may hold values from -1 to 1
- w_out: bfloat16 [512, 512], replicated, may hold values from -0.75 to 0.75
- logit_scale: float32 [8], replicated, may hold values from 1 to 400
Outputs:
- output: bfloat16 [32, 16, 32, 512], P('gx', 'gy')
- grad_input: bfloat16 [32, 16, 32, 512], P('gx', None, 'gy')
- grad_weights: float32 [2048, 512], P(('gx', 'gy'))
The draws below stay inside these ranges and needn't reach their ends.
All inputs are finite; a program needn't handle non-finite values.
Results may differ from the reference program's by a relative error of at most 0.011.
The reference program's roundings to bfloat16 on the way count: a program that leaves them out, or rounds other values in their place, can miss the bound.
Values may be sent and summed in bfloat16 or wider, within the bound.
A program may use at most 128 MiB of HBM per device.

```python
import math
import jax
import jax.numpy as jnp
from jax import lax

D = 512
HEADS = 8
HEAD_DIM = 64
NX = 32
NY = 16
NZ = 32
TOKENS = 16384


def draw_slab_tokens(key, part):
    extent = (NX, NY, NZ, D)
    values = jax.random.normal(key, extent, jnp.float32)
    return jnp.clip(values, -6.0, 6.0).astype(jnp.bfloat16)


def draw_w_qkv(key, part):
    bound = 4.0 / math.sqrt(D)
    key_first = jax.random.fold_in(key, 0)
    base = jax.random.normal(key_first, (3 * D, D), jnp.float32) / math.sqrt(D)
    return jnp.clip(base, -bound, bound).astype(jnp.bfloat16)


def draw_logit_scale(key, part):
    lowest = 1.0
    highest = 16.0
    return jnp.exp(jax.random.uniform(key, (HEADS,), jnp.float32, math.log(lowest), math.log(highest)))


def raised(array, own_key, source, target, blocks, factor):
    owner, partner = [(jnp.arange(array.shape[position]) // (array.shape[position] // blocks)).reshape([-1 if axis == position else 1 for axis in range(array.ndim)]) for position in (source, target)]
    chosen = jax.random.permutation(own_key, blocks)[partner]
    strong = (owner == chosen) | (owner == (partner + blocks // 2) % blocks)
    return jnp.where(strong, factor * array, array)


def shard_levels(rng, dims, pieces, least, top_value):
    def one(axis_at, shards_of):
        draws = jax.random.uniform(jax.random.fold_in(jax.random.fold_in(rng, 6), axis_at), (shards_of,), jnp.float32, least / len(pieces), top_value / len(pieces))
        return jnp.repeat(jnp.exp(draws), dims[axis_at] // shards_of).reshape((-1,) + (1,) * (len(dims) - axis_at - 1))

    factor_of = one(*pieces[0])
    for cut in pieces[1:]:
        factor_of = factor_of * one(*cut)
    return factor_of


def scatter_about(rng, dims, width, most, cuts=(), kind=jnp.bfloat16):
    result = width * jax.random.normal(rng, dims, jnp.float32)
    if cuts:
        result = result * shard_levels(rng, dims, cuts, -0.22, 0.18)
    return jnp.clip(result, -most, most).astype(kind)


def bell_draw_with(own_key, shape, deviation, most, cuts, heavy, kind=jnp.bfloat16):
    entries = deviation * jax.random.normal(own_key, shape, jnp.float32)
    if cuts:
        entries = entries * shard_levels(own_key, shape, cuts, -0.22, 0.18)
    return jnp.clip(raised(entries, jax.random.fold_in(own_key, 3), *heavy), -most, most).astype(kind)


def setup_inputs(seed: int = 0) -> dict:
    arg_keys = jax.random.split(jax.random.key(seed), 6)
    slab_tokens = draw_slab_tokens(jax.random.fold_in(arg_keys[5], 71), 0)
    cotangent = bell_draw_with(arg_keys[1], (NX, NY, NZ, D), 1.0, 6.0, ((0, 16), (1, 8)), (0, 3, 16, 2.0))
    w_qkv = draw_w_qkv(jax.random.fold_in(arg_keys[5], 71), 0)
    w_out = scatter_about(arg_keys[3], (D, D), (D // 8) ** -0.5, 0.75)
    logit_scale = draw_logit_scale(jax.random.fold_in(arg_keys[5], 71), 0)
    return {"slab_tokens": slab_tokens, "cotangent": cotangent, "w_qkv": w_qkv, "w_out": w_out, "logit_scale": logit_scale}


EPSILON = 1e-06
NEGATIVE = -1e+30
OFFSETS = tuple(((first, second, third) for first in range(3) for second in range(3) for third in range(3)))

def rms_rows(values):
    return values * lax.rsqrt(lax.optimization_barrier(jnp.mean(values * values, axis=-1, keepdims=True)) + EPSILON)

def head_split(values):
    return values.reshape(values.shape[:-1] + (HEADS, HEAD_DIM))

def project_heads(qkv_all, logit_scale):
    leading = qkv_all.shape[:-1]
    query_part = rms_rows(head_split(qkv_all[..., :D])) * (logit_scale / HEAD_DIM)[:, None]
    key_part = rms_rows(head_split(qkv_all[..., D:2 * D]))
    pairs = jnp.concatenate([key_part.reshape(leading + (D,)), qkv_all[..., 2 * D:]], axis=-1)
    return (query_part.reshape(leading + (D,)), pairs)

def offset_score(offset):

    def compute(queries, key_part):
        extent = queries.shape[:3]
        window = lax.slice(key_part, (offset[0], offset[1], offset[2], 0), (offset[0] + extent[0], offset[1] + extent[1], offset[2] + extent[2], key_part.shape[3]))
        return lax.optimization_barrier(jnp.sum(head_split(queries) * head_split(window), axis=-1))
    return jax.checkpoint(compute)

def offset_mix(offset):

    def compute(weights, value_part):
        extent = weights.shape[:3]
        window = lax.slice(value_part, (offset[0], offset[1], offset[2], 0), (offset[0] + extent[0], offset[1] + extent[1], offset[2] + extent[2], value_part.shape[3]))
        return (weights[..., None] * head_split(window)).reshape(extent + (D,))
    return jax.checkpoint(compute)

def attend(queries, kv_ext, start_x, start_y, total_x, total_y):
    extent = queries.shape[:3]
    key_part = kv_ext[..., :D]
    value_part = kv_ext[..., D:]
    pos_x = start_x + lax.iota(jnp.int32, extent[0])
    pos_y = start_y + lax.iota(jnp.int32, extent[1])
    pos_z = lax.iota(jnp.int32, extent[2])
    scores = []
    for offset in OFFSETS:
        flag_x = (pos_x + offset[0] - 1 >= 0) & (pos_x + offset[0] - 1 < total_x)
        flag_y = (pos_y + offset[1] - 1 >= 0) & (pos_y + offset[1] - 1 < total_y)
        flag_z = (pos_z + offset[2] - 1 >= 0) & (pos_z + offset[2] - 1 < extent[2])
        inside = flag_x[:, None, None, None] & flag_y[None, :, None, None] & flag_z[None, None, :, None]
        scores.append(jnp.where(inside, offset_score(offset)(queries, key_part), NEGATIVE))
    stacked = jnp.stack(scores)
    weights = jax.nn.softmax(stacked, axis=0)
    log_totals = jax.nn.logsumexp(stacked, axis=0)
    blended = jnp.zeros(extent + (D,), queries.dtype)
    for index, offset in enumerate(OFFSETS):
        blended = blended + offset_mix(offset)(weights[index], value_part)
    return (blended, log_totals)

def reference(slab_tokens, cotangent, w_qkv, w_out, logit_scale):
    size_x, size_y, size_z = slab_tokens.shape[:3]
    x_float = slab_tokens.astype(jnp.float32)
    normed_float, norm_back = jax.vjp(rms_rows, x_float)
    normed_rows = normed_float.astype(jnp.bfloat16).reshape(-1, D)
    qkv_all = jnp.dot(normed_rows, w_qkv.T, preferred_element_type=jnp.float32).reshape(size_x, size_y, size_z, 3 * D)
    (query_float, pair_float), head_back = jax.vjp(lambda qkv_arg: project_heads(qkv_arg, logit_scale), qkv_all)
    query_b = query_float.astype(jnp.bfloat16)
    pair_b = pair_float.astype(jnp.bfloat16)
    kv_ext = jnp.pad(pair_b, ((1, 1), (1, 1), (1, 1), (0, 0))).astype(jnp.float32)
    attended, attention_back, log_totals = jax.vjp(lambda query_arg, pair_arg: attend(query_arg, pair_arg, 0, 0, size_x, size_y), query_b.astype(jnp.float32), kv_ext, has_aux=True)
    attended_rows = attended.astype(jnp.bfloat16).reshape(-1, D)
    projected = jnp.dot(attended_rows, w_out.T, preferred_element_type=jnp.float32)
    output = (x_float + projected.reshape(x_float.shape)).astype(jnp.bfloat16)
    grad_rows = cotangent.reshape(-1, D)
    upstream = jnp.dot(grad_rows, w_out, preferred_element_type=jnp.float32).astype(jnp.bfloat16)
    grad_query, grad_ext = attention_back(upstream.reshape(x_float.shape).astype(jnp.float32))
    grad_kv = grad_ext[1:-1, 1:-1, 1:-1]
    grad_qkv, = head_back((grad_query, grad_kv))
    grad_qkv_b = grad_qkv.astype(jnp.bfloat16).reshape(-1, 3 * D)
    grad_normed = jnp.dot(grad_qkv_b, w_qkv, preferred_element_type=jnp.float32).reshape(x_float.shape)
    grad_norm_in, = norm_back(grad_normed)
    grad_input = (cotangent.astype(jnp.float32) + grad_norm_in).astype(jnp.bfloat16)
    factor = 1.0 / math.sqrt(TOKENS)
    grad_first = jnp.dot(grad_qkv_b.T, normed_rows, preferred_element_type=jnp.float32) * factor
    grad_second = jnp.dot(grad_rows.T, attended_rows, preferred_element_type=jnp.float32) * factor
    grad_weights = jnp.concatenate([grad_first, grad_second], axis=0)
    return (output, grad_input, grad_weights)
```

```python
import functools

import jax
import jax.numpy as jnp
from jax import lax
from jax.experimental import pallas as pl
from jax.experimental.pallas import tpu as pltpu
from jax.sharding import PartitionSpec as P

MESH = pl.DeviceIdType.MESH
F32 = jnp.float32
BF16 = jnp.bfloat16

D = 512
HEADS = 8
HEAD_DIM = 64
NX, NY, NZ = 32, 16, 32
GX, GY = 16, 8
CHIPS = 64
OWN = 128
EXT = 384
EPSILON = 1e-06
NEGATIVE = -1e30
FACTOR = 1.0 / 128.0

SIDES = ((-1, 0), (1, 0), (0, -1), (0, 1), (-1, -1), (-1, 1), (1, -1), (1, 1))
REGION = {
    (-1, 0): (8, 4),
    (1, 0): (12, 4),
    (0, -1): (16, 2),
    (0, 1): (18, 2),
    (-1, -1): (20, 1),
    (-1, 1): (21, 1),
    (1, -1): (22, 1),
    (1, 1): (23, 1),
}


def dot_nn(a, b):
    return jnp.dot(a, b, preferred_element_type=F32)


def dot_nt(a, b):
    return lax.dot_general(a, b, (((1,), (1,)), ((), ())), preferred_element_type=F32)


def dot_tn(a, b):
    return lax.dot_general(a, b, (((0,), (0,)), ((), ())), preferred_element_type=F32)


def iota(shape, dim):
    return lax.broadcasted_iota(jnp.int32, shape, dim)


def natural_row(r):
    return ((r >> 3) & 1) * 64 + (r & 1) * 32 + (r >> 4) * 4 + ((r >> 1) & 3)


def token_row(r):
    return ((r >> 3) & 1) * 64 + ((r >> 1) & 3) * 16 + (r >> 4) * 2 + (r & 1)


def slab_row(t):
    return ((t >> 6) & 1) * 64 + (t & 15) * 4 + ((t >> 4) & 3)


def gather_rows(index):
    shape = (OWN, OWN)
    return jnp.where(index(iota(shape, 0)) == iota(shape, 1), 1.0, 0.0).astype(BF16)


def scatter_rows(index):
    shape = (OWN, OWN)
    return jnp.where(index(iota(shape, 1)) == iota(shape, 0), 1.0, 0.0).astype(BF16)


def moved(matrix, rows):
    return dot_nn(matrix, rows).astype(BF16)


def neighbourhood_bias(gx, gy):
    shape = (EXT, OWN)
    row, col = iota(shape, 0), iota(shape, 1)
    cell, y = row >> 4, row & 15
    x = jnp.where(
        cell < 8,
        cell >> 2,
        jnp.where(
            cell < 16,
            jnp.where(cell < 12, -1, 2),
            jnp.where(cell < 20, cell & 1, jnp.where(cell < 22, -1, 2)),
        ),
    )
    z = jnp.where(
        cell < 16,
        cell & 3,
        jnp.where(
            cell < 20, jnp.where(cell < 18, -1, 4), jnp.where((cell & 1) == 0, -1, 4)
        ),
    )
    near = (
        (jnp.abs(x - (col >> 6)) <= 1)
        & (jnp.abs(z - ((col >> 4) & 3)) <= 1)
        & (jnp.abs(y - (col & 15)) <= 1)
    )
    full_x, full_z = x + 2 * gx, z + 4 * gy
    inside = (full_x >= 0) & (full_x < NX) & (full_z >= 0) & (full_z < NZ)
    return jnp.where(near & inside, 0.0, NEGATIVE)


def kernel(
    xs, cot, wqkv_hbm, wout_hbm, scale,
    out, gin, gw,
    xext, cot_send, cot_stage, wqkv, wout, normed, raw,
    q_b, k_b, v_b, q_hat, k_hat, q_inv, k_inv, u_b, att,
    gq, gk, gv, cot_tok, cot_t, bias,
    pair_send, pair_recv, half, sum_send, sum_recv,
    gn_send, gn_recv, out_send, out_stage,
    w_sem, x_ssem, x_rsem, c_ssem, c_rsem, p_ssem, p_rsem,
    a_ssem, a_rsem, g_ssem, g_rsem, o_ssem, o_rsem,
):
    gx, gy = lax.axis_index("gx"), lax.axis_index("gy")
    core = gx & 1
    chip = (gx >> 1) * GY + gy

    def exists(side):
        ok = None
        for at, step, size in ((gx, side[0], GX), (gy, side[1], GY)):
            if step:
                here = at > 0 if step < 0 else at < size - 1
                ok = here if ok is None else ok & here
        return ok

    def remote(src, dst, ssem, rsem, to_x, to_y):
        return pltpu.make_async_remote_copy(
            src_ref=src, dst_ref=dst, send_sem=ssem, recv_sem=rsem,
            device_id=(to_x, to_y), device_id_type=MESH,
        )

    def wait_for(ref, sem):
        pltpu.make_async_copy(ref, ref, sem).wait()

    load_qkv = pltpu.make_async_copy(wqkv_hbm, wqkv, w_sem.at[0])
    load_out = pltpu.make_async_copy(wout_hbm, wout, w_sem.at[1])
    load_qkv.start()
    load_out.start()

    barrier = pltpu.get_barrier_semaphore()

    def greet(k, carry):
        other = (chip + k) & (CHIPS - 1)
        pl.semaphore_signal(
            barrier, inc=1,
            device_id=((other >> 3) * 2 + core, other & 7), device_id_type=MESH,
        )
        return carry

    for side in SIDES:
        if side[0]:
            @pl.when(exists(side))
            def _():
                pl.semaphore_signal(
                    barrier, inc=1,
                    device_id=(gx + side[0], gy + side[1]), device_id_type=MESH,
                )
    lax.fori_loop(1, CHIPS, greet, 0)

    cot_send[...] = moved(gather_rows(natural_row), cot[...]).reshape(8, 16, D)
    one = jnp.int32(1)
    zero = jnp.int32(0)
    count_x = jnp.where(gx > 0, one, zero) + jnp.where(gx < GX - 1, one, zero)
    count_y = one + jnp.where(gy > 0, one, zero) + jnp.where(gy < GY - 1, one, zero)
    pl.semaphore_wait(barrier, (CHIPS - 1) + count_x * count_y)

    def border(ref, side):
        x = {-1: 0, 1: 1}.get(side[0])
        z = {-1: 0, 1: 3}.get(side[1])
        if z is None:
            return ref.at[x]
        if x is None:
            return ref.at[:, z]
        return ref.at[pl.ds(x, 1), z]

    def halo_copy(index, side):
        start, size = REGION[(-side[0], -side[1])]
        return remote(
            border(xs, side), xext.at[pl.ds(start, size)],
            x_ssem.at[index], x_rsem.at[index], gx + side[0], gy + side[1],
        )

    for index, side in enumerate(SIDES):
        @pl.when(exists(side))
        def _():
            halo_copy(index, side).start()

    def cot_copy(k, carry):
        to = (gy + k) & (GY - 1)
        remote(
            cot_send.at[to], cot_stage.at[gy], c_ssem.at[0], c_rsem.at[0], gx, to
        ).start()
        return carry

    lax.fori_loop(1, GY, cot_copy, 0)
    cot_stage[gy] = cot_send[gy]

    for side in SIDES:
        start, size = REGION[side]

        @pl.when(jnp.logical_not(exists(side)))
        def _():
            xext[pl.ds(start, size)] = jnp.zeros((size, 16, D), BF16)
            gn_recv[pl.ds(start - 8, size)] = jnp.zeros((size, 16, D), BF16)

    bias[...] = neighbourhood_bias(gx, gy)

    def rows_normed(rows):
        return rows * lax.rsqrt(jnp.mean(rows * rows, axis=-1, keepdims=True) + EPSILON)

    x_rows = xs[...].reshape(OWN, D)
    normed[0:OWN] = rows_normed(x_rows.astype(F32)).astype(BF16)
    load_qkv.wait()
    raw[:, 0:OWN] = dot_nt(wqkv[...], normed[0:OWN])

    def head_rows(base, h):
        return pl.ds(pl.multiple_of(base + h * HEAD_DIM, HEAD_DIM), HEAD_DIM)

    def head_inverse(values):
        return lax.rsqrt(jnp.mean(values * values, axis=0, keepdims=True) + EPSILON)

    def own_heads(h, carry):
        q = raw[head_rows(0, h), 0:OWN]
        inverse = head_inverse(q)
        hat = q * inverse
        q_hat[h] = hat
        q_inv[h] = inverse
        q_b[h] = (hat * (scale[h] / HEAD_DIM)).astype(BF16)
        k = raw[head_rows(D, h), 0:OWN]
        inverse = head_inverse(k)
        hat = k * inverse
        k_hat[h, :, 0:OWN] = hat
        k_inv[h, :, 0:OWN] = inverse
        k_b[h, :, 0:OWN] = hat.astype(BF16)
        v_b[h, :, 0:OWN] = raw[head_rows(2 * D, h), 0:OWN].astype(BF16)
        return carry

    lax.fori_loop(0, HEADS, own_heads, 0)

    load_out.wait()
    wait_for(cot_stage.at[pl.ds(0, GY - 1)], c_rsem.at[0])
    tokens = moved(scatter_rows(token_row), cot_stage[...].reshape(OWN, D))
    cot_tok[...] = tokens
    cot_t[...] = tokens.T.reshape(8, HEAD_DIM, OWN)
    u_b[...] = (
        dot_tn(wout[...], cot_t[...].reshape(D, OWN))
        .astype(BF16)
        .reshape(HEADS, HEAD_DIM, OWN)
    )

    for index, side in enumerate(SIDES):
        opposite = SIDES.index((-side[0], -side[1]))
        start, size = REGION[side]

        @pl.when(exists(side))
        def _():
            wait_for(xext.at[pl.ds(start, size)], x_rsem.at[opposite])

    halo_rows = xext[8:24].reshape(EXT - OWN, D)
    normed[OWN:EXT] = rows_normed(halo_rows.astype(F32)).astype(BF16)
    raw[D : 3 * D, OWN:EXT] = dot_nt(wqkv[D : 3 * D], normed[OWN:EXT])

    def halo_heads(h, carry):
        k = raw[head_rows(D, h), OWN:EXT]
        inverse = head_inverse(k)
        hat = k * inverse
        k_hat[h, :, OWN:EXT] = hat
        k_inv[h, :, OWN:EXT] = inverse
        k_b[h, :, OWN:EXT] = hat.astype(BF16)
        v_b[h, :, OWN:EXT] = raw[head_rows(2 * D, h), OWN:EXT].astype(BF16)
        return carry

    lax.fori_loop(0, HEADS, halo_heads, 0)

    def back_through(grad, hat, inverse):
        return inverse * (grad - hat * jnp.mean(grad * hat, axis=0, keepdims=True))

    def attend(h, carry):
        q, k, v, u = q_b[h], k_b[h], v_b[h], u_b[h]
        scores = dot_tn(k, q) + bias[...]
        shifted = jnp.exp(scores - jnp.max(scores, axis=0, keepdims=True))
        weights = shifted * (1.0 / jnp.sum(shifted, axis=0, keepdims=True))
        weights_b = weights.astype(BF16)
        att[h] = dot_nn(v, weights_b).astype(BF16)
        grad_w = dot_tn(v, u)
        inner = jnp.sum(weights * grad_w, axis=0, keepdims=True)
        grad_s = (weights * (grad_w - inner)).astype(BF16)
        grad_q = dot_nn(k, grad_s)
        gq[h] = (
            back_through(grad_q, q_hat[h], q_inv[h]) * (scale[h] / HEAD_DIM)
        ).astype(BF16)
        grad_k = dot_nt(q, grad_s)
        gk[h] = back_through(grad_k, k_hat[h], k_inv[h]).astype(BF16)
        gv[h] = dot_nt(u, weights_b).astype(BF16)
        return carry

    lax.fori_loop(0, HEADS, attend, 0)

    def weight_block(part, which, of_core):
        at = pl.ds((2 * which + of_core) * 2, 2)
        if part == 3:
            rows = cot_t[at].reshape(128, OWN)
            return dot_nt(rows, att[...].reshape(D, OWN))
        if part == 0:
            return dot_nn(gq[at].reshape(128, OWN), normed[0:OWN])
        return dot_nn((gk if part == 1 else gv)[at].reshape(128, EXT), normed[...])

    def pair_copy(part):
        return remote(
            pair_send.at[part], pair_recv.at[part],
            p_ssem.at[part], p_rsem.at[part], gx + 1 - 2 * core, gy,
        )

    order = (3, 0, 1, 2)
    for part in order:
        for which in range(2):
            pair_send[part, which] = weight_block(part, which, 1 - core).astype(BF16)
        pair_copy(part).start()
    for part in order:
        for which in range(2):
            half[part, which] = weight_block(part, which, core)

    grad_kv_halo = jnp.concatenate(
        [gk[:, :, OWN:EXT].reshape(D, EXT - OWN), gv[:, :, OWN:EXT].reshape(D, EXT - OWN)],
        axis=0,
    )
    gn_send[...] = (
        dot_tn(grad_kv_halo, wqkv[D : 3 * D]).astype(BF16).reshape(16, 16, D)
    )

    def grad_copy(index, side):
        start, size = REGION[side]
        target, _ = REGION[(-side[0], -side[1])]
        return remote(
            gn_send.at[pl.ds(start - 8, size)], gn_recv.at[pl.ds(target - 8, size)],
            g_ssem.at[index], g_rsem.at[index], gx + side[0], gy + side[1],
        )

    for index, side in enumerate(SIDES):
        @pl.when(exists(side))
        def _():
            grad_copy(index, side).start()

    for part in order:
        pair_copy(part).wait_recv()
        total = half[part] + pair_recv[part].astype(F32)
        sum_send[16 * part : 16 * part + 16] = total.astype(BF16).reshape(16, 16, D)

    def sum_copy(k, carry):
        other = (chip + k) & (CHIPS - 1)
        remote(
            sum_send.at[other], sum_recv.at[chip], a_ssem.at[0], a_rsem.at[0],
            (other >> 3) * 2 + core, other & 7,
        ).start()
        return carry

    lax.fori_loop(1, CHIPS, sum_copy, 0)
    sum_recv[chip] = sum_send[chip]

    projected = dot_nn(wout[...], att[...].reshape(D, OWN)).T
    out_rows = (x_rows.astype(F32) + projected).astype(BF16)
    out_send[...] = moved(gather_rows(token_row), out_rows).reshape(8, 16, D)

    def out_copy(k, carry):
        to = (gy + k) & (GY - 1)
        remote(
            out_send.at[to], out_stage.at[gy], o_ssem.at[0], o_rsem.at[0], gx, to
        ).start()
        return carry

    lax.fori_loop(1, GY, out_copy, 0)
    out_stage[gy] = out_send[gy]

    grad_own = jnp.concatenate(
        [
            gq[...].reshape(D, OWN),
            gk[:, :, 0:OWN].reshape(D, OWN),
            gv[:, :, 0:OWN].reshape(D, OWN),
        ],
        axis=0,
    )
    grad_n = dot_tn(grad_own, wqkv[...]).reshape(2, 4, 16, D)
    for index, side in enumerate(SIDES):
        opposite = SIDES.index((-side[0], -side[1]))
        start, size = REGION[side]

        @pl.when(exists(side))
        def _():
            wait_for(gn_recv.at[pl.ds(start - 8, size)], g_rsem.at[opposite])

    def term(side):
        start, size = REGION[side]
        return gn_recv[start - 8 : start - 8 + size].astype(F32)

    planes = []
    for x in range(2):
        side_x = (-1, 1)[x]
        plane = grad_n[x] + term((side_x, 0))
        low = term((0, -1))[x] + term((side_x, -1))[0]
        high = term((0, 1))[x] + term((side_x, 1))[0]
        planes.append(
            jnp.concatenate(
                [plane[0:1] + low[None], plane[1:3], plane[3:4] + high[None]], axis=0
            )
        )
    grad_n = jnp.concatenate(planes, axis=0).reshape(OWN, D)
    x_float = x_rows.astype(F32)
    inverse = lax.rsqrt(jnp.mean(x_float * x_float, axis=-1, keepdims=True) + EPSILON)
    x_hat = x_float * inverse
    grad_x = inverse * (grad_n - x_hat * jnp.mean(grad_n * x_hat, axis=-1, keepdims=True))
    grad_rows = (cot_tok[...].astype(F32) + grad_x).astype(BF16)
    gin[...] = moved(scatter_rows(slab_row), grad_rows)

    wait_for(out_stage.at[pl.ds(0, GY - 1)], o_rsem.at[0])
    out[...] = moved(scatter_rows(natural_row), out_stage[...].reshape(OWN, D))

    wait_for(sum_recv.at[pl.ds(0, CHIPS - 1)], a_rsem.at[0])
    gw[...] = jnp.sum(sum_recv[...].astype(F32), axis=0) * FACTOR

    for index, side in enumerate(SIDES):
        @pl.when(exists(side))
        def _():
            halo_copy(index, side).wait_send()
            grad_copy(index, side).wait_send()

    for part in order:
        pair_copy(part).wait_send()
    wait_for(cot_send.at[pl.ds(0, GY - 1)], c_ssem.at[0])
    wait_for(out_send.at[pl.ds(0, GY - 1)], o_ssem.at[0])
    wait_for(sum_send.at[pl.ds(0, CHIPS - 1)], a_ssem.at[0])


def on_device(slab_tokens, cotangent, w_qkv, w_out, logit_scale):
    xs = slab_tokens.transpose(0, 2, 1, 3)
    vmem = pl.BlockSpec(memory_space=pltpu.VMEM)
    hbm = pl.BlockSpec(memory_space=pl.ANY)
    smem = pl.BlockSpec(memory_space=pltpu.SMEM)
    dma = pltpu.SemaphoreType.DMA
    out, gin, gw = pl.pallas_call(
        kernel,
        out_shape=(
            jax.ShapeDtypeStruct((OWN, D), BF16),
            jax.ShapeDtypeStruct((OWN, D), BF16),
            jax.ShapeDtypeStruct((16, D), F32),
        ),
        in_specs=[vmem, vmem, hbm, hbm, smem],
        out_specs=(vmem, vmem, vmem),
        scratch_shapes=[
            pltpu.VMEM((24, 16, D), BF16),
            pltpu.VMEM((8, 16, D), BF16),
            pltpu.VMEM((8, 16, D), BF16),
            pltpu.VMEM((3 * D, D), BF16),
            pltpu.VMEM((D, D), BF16),
            pltpu.VMEM((EXT, D), BF16),
            pltpu.VMEM((3 * D, EXT), F32),
            pltpu.VMEM((HEADS, HEAD_DIM, OWN), BF16),
            pltpu.VMEM((HEADS, HEAD_DIM, EXT), BF16),
            pltpu.VMEM((HEADS, HEAD_DIM, EXT), BF16),
            pltpu.VMEM((HEADS, HEAD_DIM, OWN), F32),
            pltpu.VMEM((HEADS, HEAD_DIM, EXT), F32),
            pltpu.VMEM((HEADS, 1, OWN), F32),
            pltpu.VMEM((HEADS, 1, EXT), F32),
            pltpu.VMEM((HEADS, HEAD_DIM, OWN), BF16),
            pltpu.VMEM((HEADS, HEAD_DIM, OWN), BF16),
            pltpu.VMEM((HEADS, HEAD_DIM, OWN), BF16),
            pltpu.VMEM((HEADS, HEAD_DIM, EXT), BF16),
            pltpu.VMEM((HEADS, HEAD_DIM, EXT), BF16),
            pltpu.VMEM((OWN, D), BF16),
            pltpu.VMEM((HEADS, HEAD_DIM, OWN), BF16),
            pltpu.VMEM((EXT, OWN), F32),
            pltpu.VMEM((4, 2, 128, D), BF16),
            pltpu.VMEM((4, 2, 128, D), BF16),
            pltpu.VMEM((4, 2, 128, D), F32),
            pltpu.VMEM((CHIPS, 16, D), BF16),
            pltpu.VMEM((CHIPS, 16, D), BF16),
            pltpu.VMEM((16, 16, D), BF16),
            pltpu.VMEM((16, 16, D), BF16),
            pltpu.VMEM((8, 16, D), BF16),
            pltpu.VMEM((8, 16, D), BF16),
            dma((2,)),
            dma((8,)), dma((8,)),
            dma((1,)), dma((1,)),
            dma((4,)), dma((4,)),
            dma((1,)), dma((1,)),
            dma((8,)), dma((8,)),
            dma((1,)), dma((1,)),
        ],
        compiler_params=pltpu.CompilerParams(
            collective_id=0, has_side_effects=True, vmem_limit_bytes=40 * 2**20
        ),
    )(xs, cotangent.reshape(OWN, D), w_qkv, w_out, logit_scale)
    return out.reshape(2, 2, 32, D), gin.reshape(2, 16, 4, D), gw


def solution(mesh):
    return jax.shard_map(
        on_device,
        mesh=mesh,
        in_specs=(P("gx", None, "gy", None), P("gx", "gy", None, None), P(), P(), P()),
        out_specs=(P("gx", "gy", None, None), P("gx", None, "gy", None), P(("gx", "gy"), None)),
        check_vma=False,
    )
```

```python
import functools

import jax
import jax.numpy as jnp
from jax import lax
from jax.experimental import pallas as pl
from jax.experimental.pallas import tpu as pltpu
from jax.sharding import PartitionSpec as P

MESH = pl.DeviceIdType.MESH
F32 = jnp.float32
BF16 = jnp.bfloat16

D = 512
HEADS = 8
HEAD_DIM = 64
NX, NY, NZ = 32, 16, 32
GX, GY = 16, 8
OWN = 128
EXT = 384
EPSILON = 1e-06
NEGATIVE = -1e30
FACTOR = 1.0 / 128.0

SIDES = ((-1, 0), (1, 0), (0, -1), (0, 1), (-1, -1), (-1, 1), (1, -1), (1, 1))
REGION = {
    (-1, 0): (8, 4),
    (1, 0): (12, 4),
    (0, -1): (16, 2),
    (0, 1): (18, 2),
    (-1, -1): (20, 1),
    (-1, 1): (21, 1),
    (1, -1): (22, 1),
    (1, 1): (23, 1),
}


def dot_nn(a, b):
    return jnp.dot(a, b, preferred_element_type=F32)


def dot_nt(a, b):
    return lax.dot_general(a, b, (((1,), (1,)), ((), ())), preferred_element_type=F32)


def dot_tn(a, b):
    return lax.dot_general(a, b, (((0,), (0,)), ((), ())), preferred_element_type=F32)


def iota(shape, dim):
    return lax.broadcasted_iota(jnp.int32, shape, dim)


def natural_row(r):
    return ((r >> 3) & 1) * 64 + (r & 1) * 32 + (r >> 4) * 4 + ((r >> 1) & 3)


def token_row(r):
    return ((r >> 3) & 1) * 64 + ((r >> 1) & 3) * 16 + (r >> 4) * 2 + (r & 1)


def slab_row(t):
    return ((t >> 6) & 1) * 64 + (t & 15) * 4 + ((t >> 4) & 3)


def gather_rows(index):
    shape = (OWN, OWN)
    return jnp.where(index(iota(shape, 0)) == iota(shape, 1), 1.0, 0.0).astype(BF16)


def scatter_rows(index):
    shape = (OWN, OWN)
    return jnp.where(index(iota(shape, 1)) == iota(shape, 0), 1.0, 0.0).astype(BF16)


def moved(matrix, rows):
    return dot_nn(matrix, rows).astype(BF16)


SLOT_X = {(0, 0): 0, (0, 3): 1, (1, 0): 2, (1, 3): 3, (2, 0): 4, (3, 0): 5}
SLOT_Z = {(0, 2): 0, (1, 2): 1, (2, 2): 2, (2, 3): 3, (3, 2): 4, (3, 3): 5}
SPAN_X = ((0, 2), (2, 2), (4, 1), (5, 1))
SPAN_Z = ((0, 1), (1, 1), (2, 2), (4, 2))


def kernel(
    xs_hbm, cot_hbm, wqkv_hbm, wout_hbm, scale_hbm,
    out, gin, gw,
    xs, cot, scale, xext, cot_send, cot_stage, wqkv, wout, normed, raw,
    q_bd, k_b, v_b, k_t, v_t, q_hat, k_hat, q_inv, k_inv, u_bd, att,
    weights_f, weights_b, gq, gk, gv, cot_tok, cot_t, bias,
    pair_send, pair_recv, sx, sy, sz, rx, ry, rz, tx, ty, tz, fx, fy, fz,
    gn_send, gn_recv, out_send, out_stage,
    w_sem, x_ssem, x_rsem, c_ssem, c_rsem, p_ssem, p_rsem,
    a_ssem, a_rsem, b_ssem, b_rsem, g_ssem, g_rsem, o_ssem, o_rsem,
):
    gx, gy = lax.axis_index("gx"), lax.axis_index("gy")
    core = gx & 1
    at_y = gx >> 2
    at_x = ((gx >> 1) & 1) * 2 + (gy & 1)
    at_z = gy >> 1

    def device_at(y, x, z):
        return (y * 4 + (x >> 1) * 2 + core, z * 2 + (x & 1))

    def exists(side):
        ok = None
        for at, step, size in ((gx, side[0], GX), (gy, side[1], GY)):
            if step:
                here = at > 0 if step < 0 else at < size - 1
                ok = here if ok is None else ok & here
        return ok

    def remote(src, dst, ssem, rsem, to):
        return pltpu.make_async_remote_copy(
            src_ref=src, dst_ref=dst, send_sem=ssem, recv_sem=rsem,
            device_id=to, device_id_type=MESH,
        )

    def wait_for(ref, sem):
        pltpu.make_async_copy(ref, ref, sem).wait()

    load_cot = pltpu.make_async_copy(cot_hbm, cot, w_sem.at[0])
    load_xs = pltpu.make_async_copy(xs_hbm, xs, w_sem.at[1])
    load_scale = pltpu.make_async_copy(scale_hbm, scale, w_sem.at[2])
    load_qkv = pltpu.make_async_copy(wqkv_hbm, wqkv, w_sem.at[3])
    load_out = pltpu.make_async_copy(wout_hbm, wout, w_sem.at[4])
    load_xs.start()
    load_cot.start()
    load_scale.start()
    load_qkv.start()
    load_out.start()

    barrier = pltpu.get_barrier_semaphore()

    def greet(to):
        pl.semaphore_signal(barrier, inc=1, device_id=to, device_id_type=MESH)

    for side in SIDES:
        if side[0]:
            @pl.when(exists(side))
            def _():
                greet((gx + side[0], gy + side[1]))

    def greet_plane(k, carry):
        x, z = (at_x + (k >> 2)) & 3, (at_z + k) & 3
        greet(device_at(at_y, x, z))
        return carry

    def greet_lines(k, carry):
        y = (at_y + 1 + (k >> 2)) & 3
        greet(device_at(y, at_x, (at_z + k) & 3))

        @pl.when((k & 3) > 0)
        def _():
            greet(device_at(y, (at_x + k) & 3, at_z))

        return carry

    lax.fori_loop(1, 16, greet_plane, 0)
    lax.fori_loop(0, 12, greet_lines, 0)

    load_cot.wait()
    cot_send[...] = moved(gather_rows(natural_row), cot[...]).reshape(8, 16, D)
    load_xs.wait()
    load_scale.wait()
    one = jnp.int32(1)
    zero = jnp.int32(0)
    count_x = jnp.where(gx > 0, one, zero) + jnp.where(gx < GX - 1, one, zero)
    count_y = one + jnp.where(gy > 0, one, zero) + jnp.where(gy < GY - 1, one, zero)
    pl.semaphore_wait(barrier, 36 + count_x * count_y)

    def border(ref, side):
        x = {-1: 0, 1: 1}.get(side[0])
        z = {-1: 0, 1: 3}.get(side[1])
        if z is None:
            return ref.at[x]
        if x is None:
            return ref.at[:, z]
        return ref.at[pl.ds(x, 1), z]

    def halo_copy(index, side):
        start, size = REGION[(-side[0], -side[1])]
        return remote(
            border(xs, side), xext.at[pl.ds(start, size)],
            x_ssem.at[index], x_rsem.at[index], (gx + side[0], gy + side[1]),
        )

    for index, side in enumerate(SIDES):
        @pl.when(exists(side))
        def _():
            halo_copy(index, side).start()

    def cot_copy(k, carry):
        to = (gy + k) & (GY - 1)
        remote(
            cot_send.at[to], cot_stage.at[gy], c_ssem.at[0], c_rsem.at[0], (gx, to)
        ).start()
        return carry

    lax.fori_loop(1, GY, cot_copy, 0)
    cot_stage[gy] = cot_send[gy]

    for side in SIDES:
        start, size = REGION[side]

        @pl.when(jnp.logical_not(exists(side)))
        def _():
            xext[pl.ds(start, size)] = jnp.zeros((size, 16, D), BF16)
            gn_recv[pl.ds(start - 8, size)] = jnp.zeros((size, 16, D), BF16)

    def rows_normed(rows):
        return rows * lax.rsqrt(jnp.mean(rows * rows, axis=-1, keepdims=True) + EPSILON)

    x_rows = xs[...].reshape(OWN, D)
    normed[0:OWN] = rows_normed(x_rows.astype(F32)).astype(BF16)
    load_qkv.wait()
    raw[:, 0:OWN] = dot_nt(wqkv[...], normed[0:OWN])

    def pair_rows(base, j):
        return pl.ds(pl.multiple_of(base + j * 128, 128), 128)

    def heads_of(values):
        return values.reshape(2, HEAD_DIM, values.shape[1])

    def head_inverse(values):
        return lax.rsqrt(jnp.mean(values * values, axis=1, keepdims=True) + EPSILON)

    q_bd[...] = jnp.zeros_like(q_bd)
    u_bd[...] = jnp.zeros_like(u_bd)

    def keys_values(j, low, high):
        k = heads_of(raw[pair_rows(D, j), low:high])
        inverse = head_inverse(k)
        hat = (k * inverse).reshape(128, high - low)
        k_hat[j, :, low:high] = hat
        k_inv[j, :, :, low:high] = inverse
        hat_b = hat.astype(BF16)
        k_b[j, :, low:high] = hat_b
        k_t[j, low:high] = hat_b.T
        v = raw[pair_rows(2 * D, j), low:high].astype(BF16)
        v_b[j, :, low:high] = v
        v_t[j, low:high] = v.T

    def own_pairs(j, carry):
        q = heads_of(raw[pair_rows(0, j), 0:OWN])
        inverse = head_inverse(q)
        hat = q * inverse
        q_hat[j] = hat.reshape(128, OWN)
        q_inv[j] = inverse
        for s in range(2):
            q_bd[j, 64 * s : 64 * s + 64, 128 * s : 128 * s + 128] = (
                hat[s] * (scale[2 * j + s] / HEAD_DIM)
            ).astype(BF16)
        keys_values(j, 0, OWN)
        return carry

    lax.fori_loop(0, 4, own_pairs, 0)

    col = iota((16, OWN), 1)
    row_y = iota((16, OWN), 0)
    col_x, col_z = col >> 6, (col >> 4) & 3
    near_y = jnp.abs(row_y - (col & 15)) <= 1

    def bias_cell(cell, carry):
        x = jnp.where(
            cell < 8,
            cell >> 2,
            jnp.where(
                cell < 16,
                jnp.where(cell < 12, -1, 2),
                jnp.where(cell < 20, cell & 1, jnp.where(cell < 22, -1, 2)),
            ),
        )
        z = jnp.where(
            cell < 16,
            cell & 3,
            jnp.where(
                cell < 20, jnp.where(cell < 18, -1, 4), jnp.where((cell & 1) == 0, -1, 4)
            ),
        )
        full_x, full_z = x + 2 * gx, z + 4 * gy
        inside = (full_x >= 0) & (full_x < NX) & (full_z >= 0) & (full_z < NZ)
        x_off = jnp.where(inside, x, jnp.int32(100))
        near = near_y & (jnp.abs(x_off - col_x) <= 1) & (jnp.abs(z - col_z) <= 1)
        block = jnp.where(near, 0.0, NEGATIVE)
        rows = pl.ds(pl.multiple_of(cell * 16, 16), 16)
        bias[rows, 0:OWN] = block
        bias[rows, OWN : 2 * OWN] = block
        return carry

    lax.fori_loop(0, 24, bias_cell, 0)

    load_out.wait()
    wait_for(cot_stage.at[pl.ds(0, GY - 1)], c_rsem.at[0])
    tokens = moved(scatter_rows(token_row), cot_stage[...].reshape(OWN, D))
    cot_tok[...] = tokens
    cot_t[...] = tokens.T.reshape(4, 128, OWN)
    upstream = dot_nn(tokens, wout[...]).astype(BF16).T
    for j in range(4):
        for s in range(2):
            u_bd[j, 64 * s : 64 * s + 64, 128 * s : 128 * s + 128] = upstream[
                128 * j + 64 * s : 128 * j + 64 * s + 64
            ]

    for index, side in enumerate(SIDES):
        opposite = SIDES.index((-side[0], -side[1]))
        start, size = REGION[side]

        @pl.when(exists(side))
        def _():
            wait_for(xext.at[pl.ds(start, size)], x_rsem.at[opposite])

    halo_rows = xext[8:24].reshape(EXT - OWN, D)
    normed[OWN:EXT] = rows_normed(halo_rows.astype(F32)).astype(BF16)
    raw[D : 3 * D, OWN:EXT] = dot_nt(wqkv[D : 3 * D], normed[OWN:EXT])

    def halo_pairs(j, carry):
        keys_values(j, OWN, EXT)
        return carry

    lax.fori_loop(0, 4, halo_pairs, 0)

    def forward(j):
        scores = dot_nn(k_t[j], q_bd[j]) + bias[...]
        shifted = jnp.exp(scores - jnp.max(scores, axis=0, keepdims=True))
        weights = shifted * (1.0 / jnp.sum(shifted, axis=0, keepdims=True))
        weights_f[j] = weights
        rounded = weights.astype(BF16)
        weights_b[j] = rounded
        for s in range(2):
            rows, cols = slice(64 * s, 64 * s + 64), slice(128 * s, 128 * s + 128)
            att[j, rows] = dot_nn(v_b[j, rows], rounded[:, cols]).astype(BF16)

    def back_through(grad, hat, inverse):
        return inverse * (grad - hat * jnp.mean(grad * hat, axis=0, keepdims=True))

    def backward(j):
        grad_w = dot_nn(v_t[j], u_bd[j])
        weights = weights_f[j]
        inner = jnp.sum(weights * grad_w, axis=0, keepdims=True)
        grad_s = (weights * (grad_w - inner)).astype(BF16)
        for s in range(2):
            rows, cols = slice(64 * s, 64 * s + 64), slice(128 * s, 128 * s + 128)
            grad_q = dot_nn(k_b[j, rows], grad_s[:, cols])
            gq[j, rows] = (
                back_through(grad_q, q_hat[j, rows], q_inv[j, s])
                * (scale[2 * j + s] / HEAD_DIM)
            ).astype(BF16)
            grad_k = dot_nt(q_bd[j, rows, cols], grad_s[:, cols])
            gk[j, rows] = back_through(grad_k, k_hat[j, rows], k_inv[j, s]).astype(BF16)
            gv[j, rows] = dot_nt(u_bd[j, rows, cols], weights_b[j, :, cols]).astype(BF16)

    def weight_block(part, j):
        if part == 3:
            return dot_nt(cot_t[j], att[...].reshape(D, OWN))
        if part == 0:
            return dot_nn(gq[j], normed[0:OWN])
        return dot_nn((gk if part == 1 else gv)[j], normed[...])

    def pair_copy(part):
        return remote(
            pair_send.at[part], pair_recv.at[part],
            p_ssem.at[part], p_rsem.at[part], (gx + 1 - 2 * core, gy),
        )

    def send_other(part):
        for which in range(2):
            block = weight_block(part, 2 * which + 1 - core)
            pair_send[part, which] = block.astype(BF16)
        pair_copy(part).start()

    def sum_own(part):
        pair_copy(part).wait_recv()
        for which in range(2):
            total = weight_block(part, 2 * which + core) + pair_recv[part, which].astype(F32)
            blocks = total.astype(BF16).reshape(8, 16, D)
            for r in range(8):
                x, z = 2 * which + (r & 1), r >> 1
                for tile in range(4):
                    value = blocks[r, :, 128 * tile : 128 * tile + 128]
                    if tile == 1:
                        sy[part, x, z] = value
                    elif (part, tile) in SLOT_X:
                        sx[x, SLOT_X[part, tile], z] = value
                    else:
                        sz[z, SLOT_Z[part, tile], x] = value

    def send_lines(slots_x, slots_z):
        def step(k, carry):
            x = (at_x + k) & 3
            remote(
                sx.at[x, slots_x], rx.at[at_x, slots_x], a_ssem.at[0], a_rsem.at[0],
                device_at(at_y, x, at_z),
            ).start()
            z = (at_z + k) & 3
            remote(
                sz.at[z, slots_z], rz.at[at_z, slots_z], a_ssem.at[2], a_rsem.at[2],
                device_at(at_y, at_x, z),
            ).start()
            return carry

        lax.fori_loop(1, 4, step, 0)

    def send_y(part):
        @pl.when(at_y != part)
        def _():
            remote(
                sy.at[part], ry.at[at_y], a_ssem.at[1], a_rsem.at[1],
                device_at(part, at_x, at_z),
            ).start()

    for j in range(4):
        forward(j)
    send_other(3)
    for which in range(2):
        backward(2 * which + 1 - core)
    for part in range(3):
        send_other(part)
    sum_own(3)
    send_y(3)
    send_lines(pl.ds(5, 1), pl.ds(4, 2))
    for which in range(2):
        backward(2 * which + core)
    for part in range(3):
        sum_own(part)
        send_y(part)
    send_lines(pl.ds(0, 5), pl.ds(0, 4))

    grad_kv_halo = jnp.concatenate(
        [gk[:, :, OWN:EXT].reshape(D, EXT - OWN), gv[:, :, OWN:EXT].reshape(D, EXT - OWN)],
        axis=0,
    )
    gn_send[...] = (
        dot_tn(grad_kv_halo, wqkv[D : 3 * D]).astype(BF16).reshape(16, 16, D)
    )

    def grad_copy(index, side):
        start, size = REGION[side]
        target, _ = REGION[(-side[0], -side[1])]
        return remote(
            gn_send.at[pl.ds(start - 8, size)], gn_recv.at[pl.ds(target - 8, size)],
            g_ssem.at[index], g_rsem.at[index], (gx + side[0], gy + side[1]),
        )

    for index, side in enumerate(SIDES):
        @pl.when(exists(side))
        def _():
            grad_copy(index, side).start()

    attended = att[...].reshape(D, OWN).T
    out_rows = (x_rows.astype(F32) + dot_nt(attended, wout[...])).astype(BF16)
    out_send[...] = moved(gather_rows(token_row), out_rows).reshape(8, 16, D)

    def out_copy(k, carry):
        to = (gy + k) & (GY - 1)
        remote(
            out_send.at[to], out_stage.at[gy], o_ssem.at[0], o_rsem.at[0], (gx, to)
        ).start()
        return carry

    lax.fori_loop(1, GY, out_copy, 0)
    out_stage[gy] = out_send[gy]

    def line_sum(own, others, me):
        ry_ = own.astype(F32)
        for k in range(1, 4):
            ry_ = ry_ + others[(me + k) & 3].astype(F32)
        return ry_.astype(BF16)

    wait_for(ry.at[pl.ds(0, 3)], a_rsem.at[1])
    ty[...] = line_sum(sy[at_y], ry, at_y)

    def send_ty(k, carry):
        x, z = (at_x + (k >> 2)) & 3, (at_z + k) & 3
        remote(
            ty.at[x, z], fy.at[at_x * 4 + at_z], b_ssem.at[0], b_rsem.at[0],
            device_at(at_y, x, z),
        ).start()
        return carry

    lax.fori_loop(1, 16, send_ty, 0)
    fy[at_x * 4 + at_z] = ty[at_x, at_z]

    wait_for(rx.at[pl.ds(0, 3)], a_rsem.at[0])
    total = line_sum(sx[at_x], rx, at_x)
    for slot in range(6):
        for z in range(4):
            tx[z, slot] = total[slot, z]
    wait_for(rz.at[pl.ds(0, 3)], a_rsem.at[2])
    total = line_sum(sz[at_z], rz, at_z)
    for slot in range(6):
        for x in range(4):
            tz[x, slot] = total[slot, x]

    for y in range(4):
        first_x, n_x = SPAN_X[y]
        first_z, n_z = SPAN_Z[y]

        def send_planes(k):
            z = (at_z + k) & 3
            remote(
                tx.at[z, pl.ds(first_x, n_x)], fx.at[at_y * 4 + at_z, pl.ds(0, n_x)],
                b_ssem.at[0], b_rsem.at[0], device_at(y, at_x, z),
            ).start()
            x = (at_x + k) & 3
            remote(
                tz.at[x, pl.ds(first_z, n_z)], fz.at[at_y * 4 + at_x, pl.ds(0, n_z)],
                b_ssem.at[0], b_rsem.at[0], device_at(y, x, at_z),
            ).start()

        def step(k, carry):
            send_planes(k)
            return carry

        lax.fori_loop(1, 4, step, 0)

        @pl.when(at_y != y)
        def _():
            send_planes(0)

        @pl.when(at_y == y)
        def _():
            fx[at_y * 4 + at_z, 0:n_x] = tx[at_z, first_x : first_x + n_x]
            fz[at_y * 4 + at_x, 0:n_z] = tz[at_x, first_z : first_z + n_z]

    grad_own = jnp.concatenate(
        [
            gq[...].reshape(D, OWN),
            gk[:, :, 0:OWN].reshape(D, OWN),
            gv[:, :, 0:OWN].reshape(D, OWN),
        ],
        axis=0,
    )
    grad_n = dot_tn(grad_own, wqkv[...]).reshape(2, 4, 16, D)
    for index, side in enumerate(SIDES):
        opposite = SIDES.index((-side[0], -side[1]))
        start, size = REGION[side]

        @pl.when(exists(side))
        def _():
            wait_for(gn_recv.at[pl.ds(start - 8, size)], g_rsem.at[opposite])

    def term(side):
        start, size = REGION[side]
        return gn_recv[start - 8 : start - 8 + size].astype(F32)

    planes = []
    for x in range(2):
        side_x = (-1, 1)[x]
        plane = grad_n[x] + term((side_x, 0))
        low = term((0, -1))[x] + term((side_x, -1))[0]
        high = term((0, 1))[x] + term((side_x, 1))[0]
        planes.append(
            jnp.concatenate(
                [plane[0:1] + low[None], plane[1:3], plane[3:4] + high[None]], axis=0
            )
        )
    grad_n = jnp.concatenate(planes, axis=0).reshape(OWN, D)
    x_float = x_rows.astype(F32)
    inverse = lax.rsqrt(jnp.mean(x_float * x_float, axis=-1, keepdims=True) + EPSILON)
    x_hat = x_float * inverse
    grad_x = inverse * (grad_n - x_hat * jnp.mean(grad_n * x_hat, axis=-1, keepdims=True))
    grad_rows = (cot_tok[...].astype(F32) + grad_x).astype(BF16)
    gin[...] = moved(scatter_rows(slab_row), grad_rows)

    wait_for(out_stage.at[pl.ds(0, GY - 1)], o_rsem.at[0])
    out[...] = moved(scatter_rows(natural_row), out_stage[...].reshape(OWN, D))

    wait_for(rx.at[pl.ds(0, 3), pl.ds(0, 5)], b_rsem.at[0])

    def owned(blocks):
        return jnp.sum(blocks.astype(F32), axis=0) * FACTOR

    gw[:, 0:128] = owned(fx[:, 0])
    gw[:, 128:256] = owned(fy[...])
    gw[:, 256:384] = owned(fz[:, 0])

    @pl.when(at_y < 2)
    def _():
        gw[:, 384:512] = owned(fx[:, 1])

    @pl.when(at_y >= 2)
    def _():
        gw[:, 384:512] = owned(fz[:, 1])

    for index, side in enumerate(SIDES):
        @pl.when(exists(side))
        def _():
            halo_copy(index, side).wait_send()
            grad_copy(index, side).wait_send()

    for part in range(4):
        pair_copy(part).wait_send()
    wait_for(cot_send.at[pl.ds(0, GY - 1)], c_ssem.at[0])
    wait_for(out_send.at[pl.ds(0, GY - 1)], o_ssem.at[0])
    wait_for(rx.at[pl.ds(0, 3)], a_ssem.at[0])
    wait_for(ry.at[pl.ds(0, 3)], a_ssem.at[1])
    wait_for(rz.at[pl.ds(0, 3)], a_ssem.at[2])
    wait_for(rx.at[pl.ds(0, 3), pl.ds(0, 5)], b_ssem.at[0])


def on_device(slab_tokens, cotangent, w_qkv, w_out, logit_scale):
    xs = slab_tokens.transpose(0, 2, 1, 3)
    vmem = pl.BlockSpec(memory_space=pltpu.VMEM)
    hbm = pl.BlockSpec(memory_space=pl.ANY)
    dma = pltpu.SemaphoreType.DMA
    out, gin, gw = pl.pallas_call(
        kernel,
        out_shape=(
            jax.ShapeDtypeStruct((OWN, D), BF16),
            jax.ShapeDtypeStruct((OWN, D), BF16),
            jax.ShapeDtypeStruct((16, D), F32),
        ),
        in_specs=[hbm] * 5,
        out_specs=(vmem, vmem, vmem),
        scratch_shapes=[
            pltpu.VMEM((2, 4, 16, D), BF16),
            pltpu.VMEM((OWN, D), BF16),
            pltpu.SMEM((HEADS,), F32),
            pltpu.VMEM((24, 16, D), BF16),
            pltpu.VMEM((8, 16, D), BF16),
            pltpu.VMEM((8, 16, D), BF16),
            pltpu.VMEM((3 * D, D), BF16),
            pltpu.VMEM((D, D), BF16),
            pltpu.VMEM((EXT, D), BF16),
            pltpu.VMEM((3 * D, EXT), F32),
            pltpu.VMEM((4, 128, 2 * OWN), BF16),
            pltpu.VMEM((4, 128, EXT), BF16),
            pltpu.VMEM((4, 128, EXT), BF16),
            pltpu.VMEM((4, EXT, 128), BF16),
            pltpu.VMEM((4, EXT, 128), BF16),
            pltpu.VMEM((4, 128, OWN), F32),
            pltpu.VMEM((4, 128, EXT), F32),
            pltpu.VMEM((4, 2, 1, OWN), F32),
            pltpu.VMEM((4, 2, 1, EXT), F32),
            pltpu.VMEM((4, 128, 2 * OWN), BF16),
            pltpu.VMEM((4, 128, OWN), BF16),
            pltpu.VMEM((4, EXT, 2 * OWN), F32),
            pltpu.VMEM((4, EXT, 2 * OWN), BF16),
            pltpu.VMEM((4, 128, OWN), BF16),
            pltpu.VMEM((4, 128, EXT), BF16),
            pltpu.VMEM((4, 128, EXT), BF16),
            pltpu.VMEM((OWN, D), BF16),
            pltpu.VMEM((4, 128, OWN), BF16),
            pltpu.VMEM((EXT, 2 * OWN), F32),
            pltpu.VMEM((4, 2, 128, D), BF16),
            pltpu.VMEM((4, 2, 128, D), BF16),
            pltpu.VMEM((4, 6, 4, 16, 128), BF16),
            pltpu.VMEM((4, 4, 4, 16, 128), BF16),
            pltpu.VMEM((4, 6, 4, 16, 128), BF16),
            pltpu.VMEM((4, 6, 4, 16, 128), BF16),
            pltpu.VMEM((4, 4, 4, 16, 128), BF16),
            pltpu.VMEM((4, 6, 4, 16, 128), BF16),
            pltpu.VMEM((4, 6, 16, 128), BF16),
            pltpu.VMEM((4, 4, 16, 128), BF16),
            pltpu.VMEM((4, 6, 16, 128), BF16),
            pltpu.VMEM((16, 2, 16, 128), BF16),
            pltpu.VMEM((16, 16, 128), BF16),
            pltpu.VMEM((16, 2, 16, 128), BF16),
            pltpu.VMEM((16, 16, D), BF16),
            pltpu.VMEM((16, 16, D), BF16),
            pltpu.VMEM((8, 16, D), BF16),
            pltpu.VMEM((8, 16, D), BF16),
            dma((5,)),
            dma((8,)), dma((8,)),
            dma((1,)), dma((1,)),
            dma((4,)), dma((4,)),
            dma((3,)), dma((3,)),
            dma((1,)), dma((1,)),
            dma((8,)), dma((8,)),
            dma((1,)), dma((1,)),
        ],
        compiler_params=pltpu.CompilerParams(
            collective_id=0, has_side_effects=True, vmem_limit_bytes=60 * 2**20
        ),
    )(xs, cotangent.reshape(OWN, D), w_qkv, w_out, logit_scale)
    return out.reshape(2, 2, 32, D), gin.reshape(2, 16, 4, D), gw


def solution(mesh):
    return jax.shard_map(
        on_device,
        mesh=mesh,
        in_specs=(P("gx", None, "gy", None), P("gx", "gy", None, None), P(), P(), P()),
        out_specs=(P("gx", "gy", None, None), P("gx", None, "gy", None), P(("gx", "gy"), None)),
        check_vma=False,
    )
```

```python
import functools

import jax
import jax.numpy as jnp
from jax import lax
from jax.experimental import pallas as pl
from jax.experimental.pallas import tpu as pltpu
from jax.sharding import PartitionSpec as P

MESH = pl.DeviceIdType.MESH
F32 = jnp.float32
BF16 = jnp.bfloat16

D = 512
HEADS = 8
HEAD_DIM = 64
NX, NY, NZ = 32, 16, 32
GX, GY = 16, 8
OWN = 128
EXT = 384
EPSILON = 1e-06
NEGATIVE = -1e30
FACTOR = 1.0 / 128.0

SIDES = ((-1, 0), (1, 0), (0, -1), (0, 1), (-1, -1), (-1, 1), (1, -1), (1, 1))
REGION = {
    (-1, 0): (8, 4),
    (1, 0): (12, 4),
    (0, -1): (16, 2),
    (0, 1): (18, 2),
    (-1, -1): (20, 1),
    (-1, 1): (21, 1),
    (1, -1): (22, 1),
    (1, 1): (23, 1),
}


def dot_nn(a, b):
    return jnp.dot(a, b, preferred_element_type=F32)


def dot_nt(a, b):
    return lax.dot_general(a, b, (((1,), (1,)), ((), ())), preferred_element_type=F32)


def dot_tn(a, b):
    return lax.dot_general(a, b, (((0,), (0,)), ((), ())), preferred_element_type=F32)


def iota(shape, dim):
    return lax.broadcasted_iota(jnp.int32, shape, dim)


def natural_row(r):
    return ((r >> 3) & 1) * 64 + (r & 1) * 32 + (r >> 4) * 4 + ((r >> 1) & 3)


def token_row(r):
    return ((r >> 3) & 1) * 64 + ((r >> 1) & 3) * 16 + (r >> 4) * 2 + (r & 1)


def slab_row(t):
    return ((t >> 6) & 1) * 64 + (t & 15) * 4 + ((t >> 4) & 3)


def gather_rows(index):
    shape = (OWN, OWN)
    return jnp.where(index(iota(shape, 0)) == iota(shape, 1), 1.0, 0.0).astype(BF16)


def scatter_rows(index):
    shape = (OWN, OWN)
    return jnp.where(index(iota(shape, 1)) == iota(shape, 0), 1.0, 0.0).astype(BF16)


def moved(matrix, rows):
    return dot_nn(matrix, rows).astype(BF16)


SLOT_X = {(0, 3): 0, (1, 3): 1}
SLOT_Z = {(0, 2): 0, (1, 2): 1, (2, 2): 2, (2, 3): 3, (3, 2): 4, (3, 3): 5}
SPAN_Z = ((0, 1), (1, 1), (2, 2), (4, 2))


def kernel(
    slab_hbm, cot_hbm, wqkv_hbm, wout_hbm, scale_hbm,
    out, gin, gw,
    slab, xs, cot, scale, xext, cot_send, cot_stage, wqkv, wout, normed, raw,
    q_bd, k_b, v_b, k_t, v_t, q_hat, k_hat, q_inv, k_inv, u_bd, att,
    weights_f, weights_b, gq, gk, gv, cot_tok, cot_t, bias,
    pair_send, pair_recv, sx, sy, sz, rx, ry, rz, tx, ty, tz, fx, fy, fz,
    gn_send, gn_recv, out_send, out_stage,
    w_sem, x_ssem, x_rsem, c_ssem, c_rsem, p_ssem, p_rsem,
    a_ssem, a_rsem, b_ssem, b_rsem, g_ssem, g_rsem, o_ssem, o_rsem,
):
    gx, gy = lax.axis_index("gx"), lax.axis_index("gy")
    core = gx & 1
    at_y = gx >> 2
    at_x = ((gx >> 1) & 1) * 2 + (gy & 1)
    at_z = gy >> 1

    def device_at(y, x, z):
        return (y * 4 + (x >> 1) * 2 + core, z * 2 + (x & 1))

    def exists(side):
        ok = None
        for at, step, size in ((gx, side[0], GX), (gy, side[1], GY)):
            if step:
                here = at > 0 if step < 0 else at < size - 1
                ok = here if ok is None else ok & here
        return ok

    def remote(src, dst, ssem, rsem, to):
        return pltpu.make_async_remote_copy(
            src_ref=src, dst_ref=dst, send_sem=ssem, recv_sem=rsem,
            device_id=to, device_id_type=MESH,
        )

    def wait_for(ref, sem):
        pltpu.make_async_copy(ref, ref, sem).wait()

    load_cot = pltpu.make_async_copy(cot_hbm, cot, w_sem.at[0])
    load_slab = pltpu.make_async_copy(slab_hbm, slab, w_sem.at[1])
    load_scale = pltpu.make_async_copy(scale_hbm, scale, w_sem.at[2])
    load_qkv = pltpu.make_async_copy(wqkv_hbm, wqkv, w_sem.at[3])
    load_out = pltpu.make_async_copy(wout_hbm, wout, w_sem.at[4])
    load_slab.start()
    load_cot.start()
    load_scale.start()
    load_qkv.start()
    load_out.start()

    barrier = pltpu.get_barrier_semaphore()

    def greet(to):
        pl.semaphore_signal(barrier, inc=1, device_id=to, device_id_type=MESH)

    for side in SIDES:
        if side[0]:
            @pl.when(exists(side))
            def _():
                greet((gx + side[0], gy + side[1]))

    def greet_plane(k, carry):
        x, z = (at_x + (k >> 2)) & 3, (at_z + k) & 3
        greet(device_at(at_y, x, z))
        return carry

    def greet_lines(k, carry):
        y = (at_y + 1 + (k >> 2)) & 3
        greet(device_at(y, at_x, (at_z + k) & 3))

        @pl.when((k & 3) > 0)
        def _():
            greet(device_at(y, (at_x + k) & 3, at_z))

        return carry

    lax.fori_loop(1, 16, greet_plane, 0)
    lax.fori_loop(0, 12, greet_lines, 0)

    load_slab.wait()
    slab_rows = slab[...].astype(F32).reshape(OWN, D).astype(BF16)
    xs[...] = moved(gather_rows(slab_row), slab_rows).reshape(2, 4, 16, D)
    one = jnp.int32(1)
    zero = jnp.int32(0)
    count_x = jnp.where(gx > 0, one, zero) + jnp.where(gx < GX - 1, one, zero)
    count_y = one + jnp.where(gy > 0, one, zero) + jnp.where(gy < GY - 1, one, zero)
    pl.semaphore_wait(barrier, 36 + count_x * count_y)

    def border(ref, side):
        x = {-1: 0, 1: 1}.get(side[0])
        z = {-1: 0, 1: 3}.get(side[1])
        if z is None:
            return ref.at[x]
        if x is None:
            return ref.at[:, z]
        return ref.at[pl.ds(x, 1), z]

    def halo_copy(index, side):
        start, size = REGION[(-side[0], -side[1])]
        return remote(
            border(xs, side), xext.at[pl.ds(start, size)],
            x_ssem.at[index], x_rsem.at[index], (gx + side[0], gy + side[1]),
        )

    for index, side in enumerate(SIDES):
        @pl.when(exists(side))
        def _():
            halo_copy(index, side).start()

    load_cot.wait()
    cot_send[...] = moved(gather_rows(natural_row), cot[...]).reshape(8, 16, D)
    load_scale.wait()

    def cot_copy(k, carry):
        to = (gy + k) & (GY - 1)
        remote(
            cot_send.at[to], cot_stage.at[gy], c_ssem.at[0], c_rsem.at[0], (gx, to)
        ).start()
        return carry

    for side in SIDES:
        start, size = REGION[side]

        @pl.when(jnp.logical_not(exists(side)))
        def _():
            xext[pl.ds(start, size)] = jnp.zeros((size, 16, D), BF16)
            gn_recv[pl.ds(start - 8, size)] = jnp.zeros((size, 16, D), BF16)

    def rows_normed(rows):
        return rows * lax.rsqrt(jnp.mean(rows * rows, axis=-1, keepdims=True) + EPSILON)

    x_rows = xs[...].reshape(OWN, D)
    normed[0:OWN] = rows_normed(x_rows.astype(F32)).astype(BF16)
    load_qkv.wait()
    raw[:, 0:OWN] = dot_nt(wqkv[...], normed[0:OWN])

    def pair_rows(base, j):
        return pl.ds(pl.multiple_of(base + j * 128, 128), 128)

    def heads_of(values):
        return values.reshape(2, HEAD_DIM, values.shape[1])

    def head_inverse(values):
        return lax.rsqrt(jnp.mean(values * values, axis=1, keepdims=True) + EPSILON)

    q_bd[...] = jnp.zeros_like(q_bd)
    u_bd[...] = jnp.zeros_like(u_bd)

    def keys_values(j, low, high):
        k = heads_of(raw[pair_rows(D, j), low:high])
        inverse = head_inverse(k)
        hat = (k * inverse).reshape(128, high - low)
        k_hat[j, :, low:high] = hat
        k_inv[j, :, :, low:high] = inverse
        hat_b = hat.astype(BF16)
        k_b[j, :, low:high] = hat_b
        k_t[j, low:high] = hat_b.T
        v = raw[pair_rows(2 * D, j), low:high].astype(BF16)
        v_b[j, :, low:high] = v
        v_t[j, low:high] = v.T

    def own_pairs(j, carry):
        q = heads_of(raw[pair_rows(0, j), 0:OWN])
        inverse = head_inverse(q)
        hat = q * inverse
        q_hat[j] = hat.reshape(128, OWN)
        q_inv[j] = inverse
        for s in range(2):
            q_bd[j, 64 * s : 64 * s + 64, 128 * s : 128 * s + 128] = (
                hat[s] * (scale[2 * j + s] / HEAD_DIM)
            ).astype(BF16)
        keys_values(j, 0, OWN)
        return carry

    lax.fori_loop(0, 4, own_pairs, 0)

    col = iota((16, OWN), 1)
    row_y = iota((16, OWN), 0)
    col_x, col_z = col >> 6, (col >> 4) & 3
    near_y = jnp.abs(row_y - (col & 15)) <= 1

    def bias_cell(cell, carry):
        x = jnp.where(
            cell < 8,
            cell >> 2,
            jnp.where(
                cell < 16,
                jnp.where(cell < 12, -1, 2),
                jnp.where(cell < 20, cell & 1, jnp.where(cell < 22, -1, 2)),
            ),
        )
        z = jnp.where(
            cell < 16,
            cell & 3,
            jnp.where(
                cell < 20, jnp.where(cell < 18, -1, 4), jnp.where((cell & 1) == 0, -1, 4)
            ),
        )
        full_x, full_z = x + 2 * gx, z + 4 * gy
        inside = (full_x >= 0) & (full_x < NX) & (full_z >= 0) & (full_z < NZ)
        x_off = jnp.where(inside, x, jnp.int32(100))
        near = near_y & (jnp.abs(x_off - col_x) <= 1) & (jnp.abs(z - col_z) <= 1)
        block = jnp.where(near, 0.0, NEGATIVE)
        rows = pl.ds(pl.multiple_of(cell * 16, 16), 16)
        bias[rows, 0:OWN] = block
        bias[rows, OWN : 2 * OWN] = block
        return carry

    lax.fori_loop(0, 24, bias_cell, 0)

    for index, side in enumerate(SIDES):
        opposite = SIDES.index((-side[0], -side[1]))
        start, size = REGION[side]

        @pl.when(exists(side))
        def _():
            wait_for(xext.at[pl.ds(start, size)], x_rsem.at[opposite])

    lax.fori_loop(1, GY, cot_copy, 0)
    cot_stage[gy] = cot_send[gy]

    halo_rows = xext[8:24].reshape(EXT - OWN, D)
    normed[OWN:EXT] = rows_normed(halo_rows.astype(F32)).astype(BF16)
    raw[D : 3 * D, OWN:EXT] = dot_nt(wqkv[D : 3 * D], normed[OWN:EXT])

    def halo_pairs(j, carry):
        keys_values(j, OWN, EXT)
        return carry

    lax.fori_loop(0, 4, halo_pairs, 0)

    def forward(j):
        scores = dot_nn(k_t[j], q_bd[j]) + bias[...]
        shifted = jnp.exp(scores - jnp.max(scores, axis=0, keepdims=True))
        weights = shifted * (1.0 / jnp.sum(shifted, axis=0, keepdims=True))
        weights_f[j] = weights
        rounded = weights.astype(BF16)
        weights_b[j] = rounded
        for s in range(2):
            rows, cols = slice(64 * s, 64 * s + 64), slice(128 * s, 128 * s + 128)
            att[j, rows] = dot_nn(v_b[j, rows], rounded[:, cols]).astype(BF16)

    def back_through(grad, hat, inverse):
        return inverse * (grad - hat * jnp.mean(grad * hat, axis=0, keepdims=True))

    def backward(j):
        grad_w = dot_nn(v_t[j], u_bd[j])
        weights = weights_f[j]
        inner = jnp.sum(weights * grad_w, axis=0, keepdims=True)
        grad_s = (weights * (grad_w - inner)).astype(BF16)
        for s in range(2):
            rows, cols = slice(64 * s, 64 * s + 64), slice(128 * s, 128 * s + 128)
            grad_q = dot_nn(k_b[j, rows], grad_s[:, cols])
            gq[j, rows] = (
                back_through(grad_q, q_hat[j, rows], q_inv[j, s])
                * (scale[2 * j + s] / HEAD_DIM)
            ).astype(BF16)
            grad_k = dot_nt(q_bd[j, rows, cols], grad_s[:, cols])
            gk[j, rows] = back_through(grad_k, k_hat[j, rows], k_inv[j, s]).astype(BF16)
            gv[j, rows] = dot_nt(u_bd[j, rows, cols], weights_b[j, :, cols]).astype(BF16)

    def weight_block(part, j):
        if part == 3:
            return dot_nt(cot_t[j], att[...].reshape(D, OWN))
        if part == 0:
            return dot_nn(gq[j], normed[0:OWN])
        return dot_nn((gk if part == 1 else gv)[j], normed[...])

    def pair_copy(part):
        return remote(
            pair_send.at[part], pair_recv.at[part],
            p_ssem.at[part], p_rsem.at[part], (gx + 1 - 2 * core, gy),
        )

    def send_other(part):
        for which in range(2):
            block = weight_block(part, 2 * which + 1 - core)
            pair_send[part, which] = block.astype(BF16)
        pair_copy(part).start()

    def sum_own(part):
        pair_copy(part).wait_recv()
        for which in range(2):
            total = weight_block(part, 2 * which + core) + pair_recv[part, which].astype(F32)
            blocks = total.astype(BF16).reshape(8, 16, D)
            for r in range(8):
                x, z = 2 * which + (r & 1), r >> 1
                for tile in range(4):
                    value = blocks[r, :, 128 * tile : 128 * tile + 128]
                    if tile < 2:
                        sy[part, x, z, :, 128 * tile : 128 * tile + 128] = value
                    elif (part, tile) in SLOT_X:
                        sx[x, SLOT_X[part, tile], z] = value
                    else:
                        sz[z, SLOT_Z[part, tile], x] = value

    def send_x(k, carry):
        x = (at_x + k) & 3
        remote(
            sx.at[x], rx.at[at_x], a_ssem.at[0], a_rsem.at[0], device_at(at_y, x, at_z)
        ).start()
        return carry

    def send_z(slots):
        def step(k, carry):
            z = (at_z + k) & 3
            remote(
                sz.at[z, slots], rz.at[at_z, slots], a_ssem.at[2], a_rsem.at[2],
                device_at(at_y, at_x, z),
            ).start()
            return carry

        lax.fori_loop(1, 4, step, 0)

    def send_y(part):
        @pl.when(at_y != part)
        def _():
            remote(
                sy.at[part], ry.at[at_y], a_ssem.at[1], a_rsem.at[1],
                device_at(part, at_x, at_z),
            ).start()

    for j in range(4):
        forward(j)

    load_out.wait()
    wait_for(cot_stage.at[pl.ds(0, GY - 1)], c_rsem.at[0])
    tokens = moved(scatter_rows(token_row), cot_stage[...].reshape(OWN, D))
    cot_tok[...] = tokens
    cot_t[...] = tokens.T.reshape(4, 128, OWN)
    upstream = dot_nn(tokens, wout[...]).astype(BF16).T
    for j in range(4):
        for s in range(2):
            u_bd[j, 64 * s : 64 * s + 64, 128 * s : 128 * s + 128] = upstream[
                128 * j + 64 * s : 128 * j + 64 * s + 64
            ]

    send_other(3)
    for which in range(2):
        backward(2 * which + 1 - core)
    for part in range(3):
        send_other(part)
    sum_own(3)
    send_y(3)
    send_z(pl.ds(4, 2))
    for which in range(2):
        backward(2 * which + core)
    for part in range(3):
        sum_own(part)
        send_y(part)
    send_z(pl.ds(0, 4))
    lax.fori_loop(1, 4, send_x, 0)

    grad_kv_halo = jnp.concatenate(
        [gk[:, :, OWN:EXT].reshape(D, EXT - OWN), gv[:, :, OWN:EXT].reshape(D, EXT - OWN)],
        axis=0,
    )
    gn_send[...] = (
        dot_tn(grad_kv_halo, wqkv[D : 3 * D]).astype(BF16).reshape(16, 16, D)
    )

    def grad_copy(index, side):
        start, size = REGION[side]
        target, _ = REGION[(-side[0], -side[1])]
        return remote(
            gn_send.at[pl.ds(start - 8, size)], gn_recv.at[pl.ds(target - 8, size)],
            g_ssem.at[index], g_rsem.at[index], (gx + side[0], gy + side[1]),
        )

    for index, side in enumerate(SIDES):
        @pl.when(exists(side))
        def _():
            grad_copy(index, side).start()

    attended = att[...].reshape(D, OWN).T
    out_rows = (x_rows.astype(F32) + dot_nt(attended, wout[...])).astype(BF16)
    out_send[...] = moved(gather_rows(token_row), out_rows).reshape(8, 16, D)

    def out_copy(k, carry):
        to = (gy + k) & (GY - 1)
        remote(
            out_send.at[to], out_stage.at[gy], o_ssem.at[0], o_rsem.at[0], (gx, to)
        ).start()
        return carry

    lax.fori_loop(1, GY, out_copy, 0)
    out_stage[gy] = out_send[gy]

    def line_sum(own, others, me):
        ry_ = own.astype(F32)
        for k in range(1, 4):
            ry_ = ry_ + others[(me + k) & 3].astype(F32)
        return ry_.astype(BF16)

    wait_for(rx.at[pl.ds(0, 3)], a_rsem.at[0])
    total = line_sum(sx[at_x], rx, at_x)
    for slot in range(2):
        for z in range(4):
            tx[z, slot] = total[slot, z]

    for y in range(2):
        def send_tx(k, carry):
            z = (at_z + k) & 3
            remote(
                tx.at[z, y], fx.at[at_y * 4 + at_z],
                b_ssem.at[0], b_rsem.at[0], device_at(y, at_x, z),
            ).start()
            return carry

        lax.fori_loop(1, 4, send_tx, 0)

        @pl.when(at_y != y)
        def _():
            send_tx(0, 0)

        @pl.when(at_y == y)
        def _():
            fx[at_y * 4 + at_z] = tx[at_z, y]

    wait_for(rz.at[pl.ds(0, 3)], a_rsem.at[2])
    total = line_sum(sz[at_z], rz, at_z)
    for slot in range(6):
        for x in range(4):
            tz[x, slot] = total[slot, x]

    for y in range(4):
        first, count = SPAN_Z[y]

        def send_tz(k, carry):
            x = (at_x + k) & 3
            remote(
                tz.at[x, pl.ds(first, count)], fz.at[at_y * 4 + at_x, pl.ds(0, count)],
                b_ssem.at[0], b_rsem.at[0], device_at(y, x, at_z),
            ).start()
            return carry

        lax.fori_loop(1, 4, send_tz, 0)

        @pl.when(at_y != y)
        def _():
            send_tz(0, 0)

        @pl.when(at_y == y)
        def _():
            fz[at_y * 4 + at_x, 0:count] = tz[at_x, first : first + count]

    wait_for(ry.at[pl.ds(0, 3)], a_rsem.at[1])
    ty[...] = line_sum(sy[at_y], ry, at_y)

    def send_ty(k, carry):
        x, z = (at_x + (k >> 2)) & 3, (at_z + k) & 3
        remote(
            ty.at[x, z], fy.at[at_x * 4 + at_z], b_ssem.at[0], b_rsem.at[0],
            device_at(at_y, x, z),
        ).start()
        return carry

    lax.fori_loop(1, 16, send_ty, 0)
    fy[at_x * 4 + at_z] = ty[at_x, at_z]

    grad_own = jnp.concatenate(
        [
            gq[...].reshape(D, OWN),
            gk[:, :, 0:OWN].reshape(D, OWN),
            gv[:, :, 0:OWN].reshape(D, OWN),
        ],
        axis=0,
    )
    grad_n = dot_tn(grad_own, wqkv[...]).reshape(2, 4, 16, D)
    for index, side in enumerate(SIDES):
        opposite = SIDES.index((-side[0], -side[1]))
        start, size = REGION[side]

        @pl.when(exists(side))
        def _():
            wait_for(gn_recv.at[pl.ds(start - 8, size)], g_rsem.at[opposite])

    def term(side):
        start, size = REGION[side]
        return gn_recv[start - 8 : start - 8 + size].astype(F32)

    planes = []
    for x in range(2):
        side_x = (-1, 1)[x]
        plane = grad_n[x] + term((side_x, 0))
        low = term((0, -1))[x] + term((side_x, -1))[0]
        high = term((0, 1))[x] + term((side_x, 1))[0]
        planes.append(
            jnp.concatenate(
                [plane[0:1] + low[None], plane[1:3], plane[3:4] + high[None]], axis=0
            )
        )
    grad_n = jnp.concatenate(planes, axis=0).reshape(OWN, D)
    x_float = x_rows.astype(F32)
    inverse = lax.rsqrt(jnp.mean(x_float * x_float, axis=-1, keepdims=True) + EPSILON)
    x_hat = x_float * inverse
    grad_x = inverse * (grad_n - x_hat * jnp.mean(grad_n * x_hat, axis=-1, keepdims=True))
    grad_rows = (cot_tok[...].astype(F32) + grad_x).astype(BF16)
    gin[...] = moved(scatter_rows(slab_row), grad_rows)

    wait_for(out_stage.at[pl.ds(0, GY - 1)], o_rsem.at[0])
    out[...] = moved(scatter_rows(natural_row), out_stage[...].reshape(OWN, D))

    wait_for(rz.at[pl.ds(0, 3), pl.ds(0, 5)], b_rsem.at[0])

    def owned(blocks):
        return jnp.sum(blocks.astype(F32), axis=0) * FACTOR

    gw[:, 0:256] = owned(fy[...])
    gw[:, 256:384] = owned(fz[:, 0])

    @pl.when(at_y < 2)
    def _():
        gw[:, 384:512] = owned(fx[...])

    @pl.when(at_y >= 2)
    def _():
        gw[:, 384:512] = owned(fz[:, 1])

    for index, side in enumerate(SIDES):
        @pl.when(exists(side))
        def _():
            halo_copy(index, side).wait_send()
            grad_copy(index, side).wait_send()

    for part in range(4):
        pair_copy(part).wait_send()
    wait_for(cot_send.at[pl.ds(0, GY - 1)], c_ssem.at[0])
    wait_for(out_send.at[pl.ds(0, GY - 1)], o_ssem.at[0])
    wait_for(rx.at[pl.ds(0, 3)], a_ssem.at[0])
    wait_for(ry.at[pl.ds(0, 3)], a_ssem.at[1])
    wait_for(rz.at[pl.ds(0, 3)], a_ssem.at[2])
    wait_for(rz.at[pl.ds(0, 3), pl.ds(0, 5)], b_ssem.at[0])


def placed(out, gin, gw, out_at, gin_at, gw_at):
    out_at[...] = out[...]
    gin_at[...] = gin[...].astype(F32).reshape(2, 16, 4, D).astype(BF16)
    gw_at[...] = gw[...]


def on_device(slab_tokens, cotangent, w_qkv, w_out, logit_scale):
    vmem = pl.BlockSpec(memory_space=pltpu.VMEM)
    hbm = pl.BlockSpec(memory_space=pl.ANY)
    dma = pltpu.SemaphoreType.DMA
    out, gin, gw = pl.pallas_call(
        kernel,
        out_shape=(
            pltpu.VMEM((OWN, D), BF16),
            pltpu.VMEM((OWN, D), BF16),
            pltpu.VMEM((16, D), F32),
        ),
        in_specs=[hbm] * 5,
        out_specs=(vmem, vmem, vmem),
        scratch_shapes=[
            pltpu.VMEM((2, 16, 4, D), BF16),
            pltpu.VMEM((2, 4, 16, D), BF16),
            pltpu.VMEM((OWN, D), BF16),
            pltpu.SMEM((HEADS,), F32),
            pltpu.VMEM((24, 16, D), BF16),
            pltpu.VMEM((8, 16, D), BF16),
            pltpu.VMEM((8, 16, D), BF16),
            pltpu.VMEM((3 * D, D), BF16),
            pltpu.VMEM((D, D), BF16),
            pltpu.VMEM((EXT, D), BF16),
            pltpu.VMEM((3 * D, EXT), F32),
            pltpu.VMEM((4, 128, 2 * OWN), BF16),
            pltpu.VMEM((4, 128, EXT), BF16),
            pltpu.VMEM((4, 128, EXT), BF16),
            pltpu.VMEM((4, EXT, 128), BF16),
            pltpu.VMEM((4, EXT, 128), BF16),
            pltpu.VMEM((4, 128, OWN), F32),
            pltpu.VMEM((4, 128, EXT), F32),
            pltpu.VMEM((4, 2, 1, OWN), F32),
            pltpu.VMEM((4, 2, 1, EXT), F32),
            pltpu.VMEM((4, 128, 2 * OWN), BF16),
            pltpu.VMEM((4, 128, OWN), BF16),
            pltpu.VMEM((4, EXT, 2 * OWN), F32),
            pltpu.VMEM((4, EXT, 2 * OWN), BF16),
            pltpu.VMEM((4, 128, OWN), BF16),
            pltpu.VMEM((4, 128, EXT), BF16),
            pltpu.VMEM((4, 128, EXT), BF16),
            pltpu.VMEM((OWN, D), BF16),
            pltpu.VMEM((4, 128, OWN), BF16),
            pltpu.VMEM((EXT, 2 * OWN), F32),
            pltpu.VMEM((4, 2, 128, D), BF16),
            pltpu.VMEM((4, 2, 128, D), BF16),
            pltpu.VMEM((4, 2, 4, 16, 128), BF16),
            pltpu.VMEM((4, 4, 4, 16, 256), BF16),
            pltpu.VMEM((4, 6, 4, 16, 128), BF16),
            pltpu.VMEM((4, 2, 4, 16, 128), BF16),
            pltpu.VMEM((4, 4, 4, 16, 256), BF16),
            pltpu.VMEM((4, 6, 4, 16, 128), BF16),
            pltpu.VMEM((4, 2, 16, 128), BF16),
            pltpu.VMEM((4, 4, 16, 256), BF16),
            pltpu.VMEM((4, 6, 16, 128), BF16),
            pltpu.VMEM((16, 16, 128), BF16),
            pltpu.VMEM((16, 16, 256), BF16),
            pltpu.VMEM((16, 2, 16, 128), BF16),
            pltpu.VMEM((16, 16, D), BF16),
            pltpu.VMEM((16, 16, D), BF16),
            pltpu.VMEM((8, 16, D), BF16),
            pltpu.VMEM((8, 16, D), BF16),
            dma((5,)),
            dma((8,)), dma((8,)),
            dma((1,)), dma((1,)),
            dma((4,)), dma((4,)),
            dma((3,)), dma((3,)),
            dma((1,)), dma((1,)),
            dma((8,)), dma((8,)),
            dma((1,)), dma((1,)),
        ],
        compiler_params=pltpu.CompilerParams(
            collective_id=0, has_side_effects=True, vmem_limit_bytes=57 * 2**20
        ),
    )(slab_tokens, cotangent.reshape(OWN, D), w_qkv, w_out, logit_scale)
    out, gin, gw = pl.pallas_call(
        placed,
        out_shape=(
            jax.ShapeDtypeStruct((OWN, D), BF16),
            jax.ShapeDtypeStruct((2, 16, 4, D), BF16),
            jax.ShapeDtypeStruct((16, D), F32),
        ),
        in_specs=[vmem] * 3,
        out_specs=(vmem,) * 3,
        compiler_params=pltpu.CompilerParams(vmem_limit_bytes=8 * 2**20),
    )(out, gin, gw)
    return out.reshape(2, 2, 32, D), gin, gw


def solution(mesh):
    return jax.shard_map(
        on_device,
        mesh=mesh,
        in_specs=(P("gx", None, "gy", None), P("gx", "gy", None, None), P(), P(), P()),
        out_specs=(P("gx", "gy", None, None), P("gx", None, "gy", None), P(("gx", "gy"), None)),
        check_vma=False,
    )
```

```python
import functools

import jax
import jax.numpy as jnp
from jax import lax
from jax.experimental import pallas as pl
from jax.experimental.pallas import tpu as pltpu
from jax.sharding import PartitionSpec as P

MESH = pl.DeviceIdType.MESH
F32 = jnp.float32
BF16 = jnp.bfloat16

D = 512
HEADS = 8
HEAD_DIM = 64
NX, NY, NZ = 32, 16, 32
GX, GY = 16, 8
OWN = 128
EXT = 384
EPSILON = 1e-06
NEGATIVE = -1e30
FACTOR = 1.0 / 128.0

SIDES = ((-1, 0), (1, 0), (0, -1), (0, 1), (-1, -1), (-1, 1), (1, -1), (1, 1))
REGION = {
    (-1, 0): (8, 4),
    (1, 0): (12, 4),
    (0, -1): (16, 2),
    (0, 1): (18, 2),
    (-1, -1): (20, 1),
    (-1, 1): (21, 1),
    (1, -1): (22, 1),
    (1, 1): (23, 1),
}


def dot_nn(a, b):
    return jnp.dot(a, b, preferred_element_type=F32)


def dot_nt(a, b):
    return lax.dot_general(a, b, (((1,), (1,)), ((), ())), preferred_element_type=F32)


def dot_tn(a, b):
    return lax.dot_general(a, b, (((0,), (0,)), ((), ())), preferred_element_type=F32)


def iota(shape, dim):
    return lax.broadcasted_iota(jnp.int32, shape, dim)


def natural_row(r):
    return ((r >> 3) & 1) * 64 + (r & 1) * 32 + (r >> 4) * 4 + ((r >> 1) & 3)


def token_row(r):
    return ((r >> 3) & 1) * 64 + ((r >> 1) & 3) * 16 + (r >> 4) * 2 + (r & 1)


def slab_row(t):
    return ((t >> 6) & 1) * 64 + (t & 15) * 4 + ((t >> 4) & 3)


def gather_rows(index):
    shape = (OWN, OWN)
    return jnp.where(index(iota(shape, 0)) == iota(shape, 1), 1.0, 0.0).astype(BF16)


def scatter_rows(index):
    shape = (OWN, OWN)
    return jnp.where(index(iota(shape, 1)) == iota(shape, 0), 1.0, 0.0).astype(BF16)


def moved(matrix, rows):
    return dot_nn(matrix, rows).astype(BF16)


SLOT_X = {(0, 1): 0, (0, 3): 1, (1, 1): 2, (2, 1): 3, (3, 0): 4, (3, 1): 5}
SLOT_Z = {(0, 2): 0, (1, 2): 1, (1, 3): 2, (2, 2): 3, (2, 3): 4, (3, 2): 5, (3, 3): 6}
SPAN_X = ((0, 2), (2, 1), (3, 1), (4, 2))
SPAN_Z = ((0, 1), (1, 2), (3, 2), (5, 2))


def kernel(
    slab_hbm, cot_hbm, wqkv_hbm, wout_hbm, scale_hbm,
    out, gin, gw,
    slab, xs, cot, scale, xext, cot_send, cot_stage, wqkv, wout, normed, raw,
    q_bd, k_b, v_b, k_t, v_t, q_hat, k_hat, q_inv, k_inv, u_bd, att,
    weights_f, weights_b, inverse, grad_f, grad_b, gq, gk, gv, cot_tok, cot_t, bias,
    pair_send, pair_recv, sx, sy, sz, rx, ry, rz, tx, ty, tz, fx, fy, fz,
    gn_send, gn_recv, out_send, out_stage,
    w_sem, x_ssem, x_rsem, c_ssem, c_rsem, p_ssem, p_rsem,
    a_ssem, a_rsem, b_ssem, b_rsem, g_ssem, g_rsem, o_ssem, o_rsem,
):
    gx, gy = lax.axis_index("gx"), lax.axis_index("gy")
    core = gx & 1
    at_y = gx >> 2
    at_x = ((gx >> 1) & 1) * 2 + (gy & 1)
    at_z = gy >> 1

    def device_at(y, x, z):
        return (y * 4 + (x >> 1) * 2 + core, z * 2 + (x & 1))

    def exists(side):
        ok = None
        for at, step, size in ((gx, side[0], GX), (gy, side[1], GY)):
            if step:
                here = at > 0 if step < 0 else at < size - 1
                ok = here if ok is None else ok & here
        return ok

    def remote(src, dst, ssem, rsem, to):
        return pltpu.make_async_remote_copy(
            src_ref=src, dst_ref=dst, send_sem=ssem, recv_sem=rsem,
            device_id=to, device_id_type=MESH,
        )

    def wait_for(ref, sem):
        pltpu.make_async_copy(ref, ref, sem).wait()

    load_cot = pltpu.make_async_copy(cot_hbm, cot, w_sem.at[0])
    load_slab = pltpu.make_async_copy(slab_hbm, slab, w_sem.at[1])
    load_scale = pltpu.make_async_copy(scale_hbm, scale, w_sem.at[2])
    load_qkv = pltpu.make_async_copy(wqkv_hbm, wqkv, w_sem.at[3])
    load_out = pltpu.make_async_copy(wout_hbm, wout, w_sem.at[4])
    load_slab.start()
    load_cot.start()
    load_scale.start()
    load_qkv.start()
    load_out.start()

    barrier = pltpu.get_barrier_semaphore()

    def greet(to):
        pl.semaphore_signal(barrier, inc=1, device_id=to, device_id_type=MESH)

    for side in SIDES:
        if side[0]:
            @pl.when(exists(side))
            def _():
                greet((gx + side[0], gy + side[1]))

    def greet_plane(k, carry):
        x, z = (at_x + (k >> 2)) & 3, (at_z + k) & 3
        greet(device_at(at_y, x, z))
        return carry

    def greet_lines(k, carry):
        y = (at_y + 1 + (k >> 2)) & 3
        greet(device_at(y, at_x, (at_z + k) & 3))

        @pl.when((k & 3) > 0)
        def _():
            greet(device_at(y, (at_x + k) & 3, at_z))

        return carry

    lax.fori_loop(1, 16, greet_plane, 0)
    lax.fori_loop(0, 12, greet_lines, 0)

    load_slab.wait()
    slab_rows = slab[...].astype(F32).reshape(OWN, D).astype(BF16)
    xs[...] = moved(gather_rows(slab_row), slab_rows).reshape(2, 4, 16, D)
    one = jnp.int32(1)
    zero = jnp.int32(0)
    count_x = jnp.where(gx > 0, one, zero) + jnp.where(gx < GX - 1, one, zero)
    count_y = one + jnp.where(gy > 0, one, zero) + jnp.where(gy < GY - 1, one, zero)
    pl.semaphore_wait(barrier, 36 + count_x * count_y)

    def border(ref, side):
        x = {-1: 0, 1: 1}.get(side[0])
        z = {-1: 0, 1: 3}.get(side[1])
        if z is None:
            return ref.at[x]
        if x is None:
            return ref.at[:, z]
        return ref.at[pl.ds(x, 1), z]

    def halo_copy(index, side):
        start, size = REGION[(-side[0], -side[1])]
        return remote(
            border(xs, side), xext.at[pl.ds(start, size)],
            x_ssem.at[index], x_rsem.at[index], (gx + side[0], gy + side[1]),
        )

    for index, side in enumerate(SIDES):
        @pl.when(exists(side))
        def _():
            halo_copy(index, side).start()

    load_cot.wait()
    cot_send[...] = moved(gather_rows(natural_row), cot[...]).reshape(8, 16, D)
    load_scale.wait()

    def cot_copy(k, carry):
        to = (gy + k) & (GY - 1)
        remote(
            cot_send.at[to], cot_stage.at[gy], c_ssem.at[0], c_rsem.at[0], (gx, to)
        ).start()
        return carry

    for side in SIDES:
        start, size = REGION[side]

        @pl.when(jnp.logical_not(exists(side)))
        def _():
            xext[pl.ds(start, size)] = jnp.zeros((size, 16, D), BF16)
            gn_recv[pl.ds(start - 8, size)] = jnp.zeros((size, 16, D), BF16)

    def rows_normed(rows):
        return rows * lax.rsqrt(jnp.mean(rows * rows, axis=-1, keepdims=True) + EPSILON)

    x_rows = xs[...].reshape(OWN, D)
    normed[0:OWN] = rows_normed(x_rows.astype(F32)).astype(BF16)
    load_qkv.wait()
    raw[:, 0:OWN] = dot_nt(wqkv[...], normed[0:OWN])

    def pair_rows(base, j):
        return pl.ds(pl.multiple_of(base + j * 128, 128), 128)

    def heads_of(values):
        return values.reshape(2, HEAD_DIM, values.shape[1])

    def head_inverse(values):
        return lax.rsqrt(jnp.mean(values * values, axis=1, keepdims=True) + EPSILON)

    q_bd[...] = jnp.zeros_like(q_bd)
    u_bd[...] = jnp.zeros_like(u_bd)

    def keys_values(j, low, high):
        k = heads_of(raw[pair_rows(D, j), low:high])
        rms = head_inverse(k)
        hat = (k * rms).reshape(128, high - low)
        k_hat[j, :, low:high] = hat
        k_inv[j, :, :, low:high] = rms
        hat_b = hat.astype(BF16)
        k_b[j, :, low:high] = hat_b
        k_t[j, low:high] = hat_b.T
        v = raw[pair_rows(2 * D, j), low:high].astype(BF16)
        v_b[j, :, low:high] = v
        v_t[j, low:high] = v.T

    def own_pairs(j, carry):
        q = heads_of(raw[pair_rows(0, j), 0:OWN])
        rms = head_inverse(q)
        hat = q * rms
        q_hat[j] = hat.reshape(128, OWN)
        q_inv[j] = rms
        for s in range(2):
            q_bd[j, 64 * s : 64 * s + 64, 128 * s : 128 * s + 128] = (
                hat[s] * (scale[2 * j + s] / HEAD_DIM)
            ).astype(BF16)
        keys_values(j, 0, OWN)
        return carry

    lax.fori_loop(0, 4, own_pairs, 0)

    col = iota((16, OWN), 1)
    row_y = iota((16, OWN), 0)
    col_x, col_z = col >> 6, (col >> 4) & 3
    near_y = jnp.abs(row_y - (col & 15)) <= 1

    def bias_cell(cell, carry):
        x = jnp.where(
            cell < 8,
            cell >> 2,
            jnp.where(
                cell < 16,
                jnp.where(cell < 12, -1, 2),
                jnp.where(cell < 20, cell & 1, jnp.where(cell < 22, -1, 2)),
            ),
        )
        z = jnp.where(
            cell < 16,
            cell & 3,
            jnp.where(
                cell < 20, jnp.where(cell < 18, -1, 4), jnp.where((cell & 1) == 0, -1, 4)
            ),
        )
        full_x, full_z = x + 2 * gx, z + 4 * gy
        inside = (full_x >= 0) & (full_x < NX) & (full_z >= 0) & (full_z < NZ)
        x_off = jnp.where(inside, x, jnp.int32(100))
        near = near_y & (jnp.abs(x_off - col_x) <= 1) & (jnp.abs(z - col_z) <= 1)
        block = jnp.where(near, 0.0, NEGATIVE)
        rows = pl.ds(pl.multiple_of(cell * 16, 16), 16)
        bias[rows, 0:OWN] = block
        bias[rows, OWN : 2 * OWN] = block
        return carry

    lax.fori_loop(0, 24, bias_cell, 0)

    lax.fori_loop(1, GY, cot_copy, 0)
    cot_stage[gy] = cot_send[gy]

    for index, side in enumerate(SIDES):
        opposite = SIDES.index((-side[0], -side[1]))
        start, size = REGION[side]

        @pl.when(exists(side))
        def _():
            wait_for(xext.at[pl.ds(start, size)], x_rsem.at[opposite])

    halo_rows = xext[8:24].reshape(EXT - OWN, D)
    normed[OWN:EXT] = rows_normed(halo_rows.astype(F32)).astype(BF16)
    raw[D : 3 * D, OWN:EXT] = dot_nt(wqkv[D : 3 * D], normed[OWN:EXT])

    def halo_pairs(j, carry):
        keys_values(j, OWN, EXT)
        return carry

    lax.fori_loop(0, 4, halo_pairs, 0, unroll=4)

    steps = [slice(low, low + 128) for low in range(0, EXT, 128)]
    halves = [(slice(64 * s, 64 * s + 64), slice(128 * s, 128 * s + 128)) for s in range(2)]

    def score_step(j, rows, top):
        scores = dot_nn(k_t[j, rows], q_bd[j]) + bias[rows]
        weights_f[j, rows] = scores
        here = jnp.max(scores, axis=0, keepdims=True)
        return here if top is None else jnp.maximum(top, here)

    def exp_step(j, rows, top, total):
        shifted = jnp.exp(weights_f[j, rows] - top)
        weights_f[j, rows] = shifted
        weights_b[j, rows] = shifted.astype(BF16)
        here = jnp.sum(shifted, axis=0, keepdims=True)
        return here if total is None else total + here

    def attend(j, total):
        scaled = 1.0 / total
        inverse[j] = scaled
        for rows, cols in halves:
            att[j, rows] = (
                dot_nn(v_b[j, rows], weights_b[j, :, cols]) * scaled[:, cols]
            ).astype(BF16)

    def forward_pairs():
        tops = [None] * 5
        for j in range(5):
            total = None
            for rows in steps:
                if j < 4:
                    tops[j] = score_step(j, rows, tops[j])
                if j:
                    total = exp_step(j - 1, rows, tops[j - 1], total)
            if j:
                attend(j - 1, total)

    def back_through(grad, hat, inverse_rms):
        return inverse_rms * (grad - hat * jnp.mean(grad * hat, axis=0, keepdims=True))

    def grad_weight_step(j, t, rows, inner):
        grad_w = dot_nn(v_t[j, rows], u_bd[j])
        grad_f[t, rows] = grad_w
        here = jnp.sum(weights_f[j, rows] * grad_w, axis=0, keepdims=True)
        return here if inner is None else inner + here

    def grad_score_step(j, t, rows, inner):
        scaled = inverse[j]
        grad_b[t, rows] = (
            weights_f[j, rows] * ((grad_f[t, rows] - inner * scaled) * scaled)
        ).astype(BF16)

    def grad_heads(j, t, s):
        rows, cols = halves[s]
        grad_q = dot_nn(k_b[j, rows], grad_b[t, :, cols])
        gq[j, rows] = (
            back_through(grad_q, q_hat[j, rows], q_inv[j, s]) * (scale[2 * j + s] / HEAD_DIM)
        ).astype(BF16)
        grad_k = dot_nt(q_bd[j, rows, cols], grad_b[t, :, cols])
        gk[j, rows] = back_through(grad_k, k_hat[j, rows], k_inv[j, s]).astype(BF16)
        up = (u_bd[j, rows, cols].astype(F32) * inverse[j][:, cols]).astype(BF16)
        gv[j, rows] = dot_nt(up, weights_b[j, :, cols]).astype(BF16)

    def backward_pairs(first, second):
        inner = [None, None]
        for rows in steps:
            inner[0] = grad_weight_step(first, 0, rows, inner[0])
        for rows in steps:
            inner[1] = grad_weight_step(second, 1, rows, inner[1])
            grad_score_step(first, 0, rows, inner[0])
        grad_heads(first, 0, 0)
        for rows in steps:
            grad_score_step(second, 1, rows, inner[1])
        grad_heads(first, 0, 1)
        for s in range(2):
            grad_heads(second, 1, s)

    def weight_block(part, j):
        if part == 3:
            return dot_nt(cot_t[j], att[...].reshape(D, OWN))
        if part == 0:
            return dot_nn(gq[j], normed[0:OWN])
        return dot_nn((gk if part == 1 else gv)[j], normed[...])

    def pair_copy(part):
        return remote(
            pair_send.at[part], pair_recv.at[part],
            p_ssem.at[part], p_rsem.at[part], (gx + 1 - 2 * core, gy),
        )

    def send_other(part):
        for which in range(2):
            block = weight_block(part, 2 * which + 1 - core)
            pair_send[part, which] = block.astype(BF16)
        pair_copy(part).start()

    def sum_own(part):
        pair_copy(part).wait_recv()
        for which in range(2):
            total = weight_block(part, 2 * which + core) + pair_recv[part, which].astype(F32)
            blocks = total.astype(BF16).reshape(8, 16, D)
            for r in range(8):
                x, z = 2 * which + (r & 1), r >> 1
                for tile in range(4):
                    value = blocks[r, :, 128 * tile : 128 * tile + 128]
                    if (part, tile) in SLOT_X:
                        sx[x, SLOT_X[part, tile], z] = value
                    elif (part, tile) in SLOT_Z:
                        sz[z, SLOT_Z[part, tile], x] = value
                    else:
                        sy[part, x, z] = value

    def send_lines(slots_x, slots_z):
        def step(k, carry):
            z = (at_z + k) & 3
            remote(
                sz.at[z, slots_z], rz.at[at_z, slots_z], a_ssem.at[2], a_rsem.at[2],
                device_at(at_y, at_x, z),
            ).start()
            x = (at_x + k) & 3
            remote(
                sx.at[x, slots_x], rx.at[at_x, slots_x], a_ssem.at[0], a_rsem.at[0],
                device_at(at_y, x, at_z),
            ).start()
            return carry

        lax.fori_loop(1, 4, step, 0)

    def send_y(part):
        @pl.when(at_y != part)
        def _():
            remote(
                sy.at[part], ry.at[at_y], a_ssem.at[1], a_rsem.at[1],
                device_at(part, at_x, at_z),
            ).start()

    forward_pairs()

    load_out.wait()
    wait_for(cot_stage.at[pl.ds(0, GY - 1)], c_rsem.at[0])
    tokens = moved(scatter_rows(token_row), cot_stage[...].reshape(OWN, D))
    cot_tok[...] = tokens
    cot_t[...] = tokens.T.reshape(4, 128, OWN)
    upstream = dot_nn(tokens, wout[...]).astype(BF16).T
    for j in range(4):
        for s in range(2):
            u_bd[j, 64 * s : 64 * s + 64, 128 * s : 128 * s + 128] = upstream[
                128 * j + 64 * s : 128 * j + 64 * s + 64
            ]

    send_other(3)
    attended = att[...].reshape(D, OWN).T
    out_rows = (x_rows.astype(F32) + dot_nt(attended, wout[...])).astype(BF16)
    out_send[...] = moved(gather_rows(token_row), out_rows).reshape(8, 16, D)

    def out_copy(k, carry):
        to = (gy + k) & (GY - 1)
        remote(
            out_send.at[to], out_stage.at[gy], o_ssem.at[0], o_rsem.at[0], (gx, to)
        ).start()
        return carry

    lax.fori_loop(1, GY, out_copy, 0)
    out_stage[gy] = out_send[gy]

    backward_pairs(1 - core, 3 - core)
    for part in range(3):
        send_other(part)
    sum_own(3)
    send_lines(pl.ds(4, 2), pl.ds(5, 2))
    backward_pairs(core, 2 + core)
    for part in range(3):
        sum_own(part)
        send_y(part)
    send_lines(pl.ds(0, 4), pl.ds(0, 5))

    grad_kv_halo = jnp.concatenate(
        [gk[:, :, OWN:EXT].reshape(D, EXT - OWN), gv[:, :, OWN:EXT].reshape(D, EXT - OWN)],
        axis=0,
    )
    gn_send[...] = (
        dot_tn(grad_kv_halo, wqkv[D : 3 * D]).astype(BF16).reshape(16, 16, D)
    )

    def grad_copy(index, side):
        start, size = REGION[side]
        target, _ = REGION[(-side[0], -side[1])]
        return remote(
            gn_send.at[pl.ds(start - 8, size)], gn_recv.at[pl.ds(target - 8, size)],
            g_ssem.at[index], g_rsem.at[index], (gx + side[0], gy + side[1]),
        )

    for index, side in enumerate(SIDES):
        @pl.when(exists(side))
        def _():
            grad_copy(index, side).start()

    wait_for(out_stage.at[pl.ds(0, GY - 1)], o_rsem.at[0])
    out[...] = moved(scatter_rows(natural_row), out_stage[...].reshape(OWN, D))

    def line_sum(own, others, me):
        ry_ = own.astype(F32)
        for k in range(1, 4):
            ry_ = ry_ + others[(me + k) & 3].astype(F32)
        return ry_.astype(BF16)

    @pl.when(at_y < 3)
    def _():
        wait_for(ry.at[pl.ds(0, 3)], a_rsem.at[1])
        ty[...] = line_sum(sy[at_y], ry, at_y)

        def send_ty(k, carry):
            x, z = (at_x + (k >> 2)) & 3, (at_z + k) & 3
            remote(
                ty.at[x, z], fy.at[at_x * 4 + at_z], b_ssem.at[0], b_rsem.at[0],
                device_at(at_y, x, z),
            ).start()
            return carry

        lax.fori_loop(1, 16, send_ty, 0)
        fy[at_x * 4 + at_z] = ty[at_x, at_z]

    def second_step(line, own, others, me, sums, spans, landing, sem, target):
        wait_for(others.at[pl.ds(0, 3)], sem)
        total = line_sum(own[me], others, me)
        for slot in range(total.shape[0]):
            for at in range(4):
                sums[at, slot] = total[slot, at]
        for y in range(4):
            first, count = spans[y]

            def send(k, carry):
                to = (line + k) & 3
                remote(
                    sums.at[to, pl.ds(first, count)],
                    landing.at[at_y * 4 + line, pl.ds(0, count)],
                    b_ssem.at[0], b_rsem.at[0], target(y, to),
                ).start()
                return carry

            lax.fori_loop(1, 4, send, 0)

            @pl.when(at_y != y)
            def _():
                send(0, 0)

            @pl.when(at_y == y)
            def _():
                landing[at_y * 4 + line, 0:count] = sums[line, first : first + count]

    second_step(
        at_z, sx, rx, at_x, tx, SPAN_X, fx, a_rsem.at[0], lambda y, z: device_at(y, at_x, z)
    )
    second_step(
        at_x, sz, rz, at_z, tz, SPAN_Z, fz, a_rsem.at[2], lambda y, x: device_at(y, x, at_z)
    )

    grad_own = jnp.concatenate(
        [
            gq[...].reshape(D, OWN),
            gk[:, :, 0:OWN].reshape(D, OWN),
            gv[:, :, 0:OWN].reshape(D, OWN),
        ],
        axis=0,
    )
    grad_n = dot_tn(grad_own, wqkv[...]).reshape(2, 4, 16, D)
    for index, side in enumerate(SIDES):
        opposite = SIDES.index((-side[0], -side[1]))
        start, size = REGION[side]

        @pl.when(exists(side))
        def _():
            wait_for(gn_recv.at[pl.ds(start - 8, size)], g_rsem.at[opposite])

    def term(side):
        start, size = REGION[side]
        return gn_recv[start - 8 : start - 8 + size].astype(F32)

    planes = []
    for x in range(2):
        side_x = (-1, 1)[x]
        plane = grad_n[x] + term((side_x, 0))
        low = term((0, -1))[x] + term((side_x, -1))[0]
        high = term((0, 1))[x] + term((side_x, 1))[0]
        planes.append(
            jnp.concatenate(
                [plane[0:1] + low[None], plane[1:3], plane[3:4] + high[None]], axis=0
            )
        )
    grad_n = jnp.concatenate(planes, axis=0).reshape(OWN, D)
    x_float = x_rows.astype(F32)
    x_inv = lax.rsqrt(jnp.mean(x_float * x_float, axis=-1, keepdims=True) + EPSILON)
    x_hat = x_float * x_inv
    grad_x = x_inv * (grad_n - x_hat * jnp.mean(grad_n * x_hat, axis=-1, keepdims=True))
    grad_rows = (cot_tok[...].astype(F32) + grad_x).astype(BF16)
    gin[...] = moved(scatter_rows(slab_row), grad_rows)

    wait_for(rz.at[pl.ds(0, 3), pl.ds(0, 5)], b_rsem.at[0])

    def put(tile, blocks):
        gw[:, 128 * tile : 128 * tile + 128] = jnp.sum(blocks.astype(F32), axis=0) * FACTOR

    @pl.when(at_y < 3)
    def _():
        put(0, fy[...])
        put(1, fx[:, 0])

    @pl.when(at_y == 3)
    def _():
        put(0, fx[:, 0])
        put(1, fx[:, 1])

    put(2, fz[:, 0])

    @pl.when(at_y == 0)
    def _():
        put(3, fx[:, 1])

    @pl.when(at_y > 0)
    def _():
        put(3, fz[:, 1])

    for index, side in enumerate(SIDES):
        @pl.when(exists(side))
        def _():
            halo_copy(index, side).wait_send()
            grad_copy(index, side).wait_send()

    for part in range(4):
        pair_copy(part).wait_send()
    wait_for(cot_send.at[pl.ds(0, GY - 1)], c_ssem.at[0])
    wait_for(out_send.at[pl.ds(0, GY - 1)], o_ssem.at[0])
    wait_for(rx.at[pl.ds(0, 3)], a_ssem.at[0])
    wait_for(rz.at[pl.ds(0, 3)], a_ssem.at[2])

    @pl.when(at_y < 3)
    def _():
        wait_for(ry.at[pl.ds(0, 2)], a_ssem.at[1])
        wait_for(rz.at[pl.ds(0, 4), pl.ds(0, 4)], b_ssem.at[0])

    @pl.when(at_y == 3)
    def _():
        wait_for(ry.at[pl.ds(0, 3)], a_ssem.at[1])
        wait_for(rz.at[pl.ds(0, 3), pl.ds(0, 4)], b_ssem.at[0])


def placed(out, gin, gw, out_at, gin_at, gw_at):
    out_at[...] = out[...]
    gin_at[...] = gin[...].astype(F32).reshape(2, 16, 4, D).astype(BF16)
    gw_at[...] = gw[...]


def on_device(slab_tokens, cotangent, w_qkv, w_out, logit_scale):
    vmem = pl.BlockSpec(memory_space=pltpu.VMEM)
    hbm = pl.BlockSpec(memory_space=pl.ANY)
    dma = pltpu.SemaphoreType.DMA
    out, gin, gw = pl.pallas_call(
        kernel,
        out_shape=(
            pltpu.VMEM((OWN, D), BF16),
            pltpu.VMEM((OWN, D), BF16),
            pltpu.VMEM((16, D), F32),
        ),
        in_specs=[hbm] * 5,
        out_specs=(vmem, vmem, vmem),
        scratch_shapes=[
            pltpu.VMEM((2, 16, 4, D), BF16),
            pltpu.VMEM((2, 4, 16, D), BF16),
            pltpu.VMEM((OWN, D), BF16),
            pltpu.SMEM((HEADS,), F32),
            pltpu.VMEM((24, 16, D), BF16),
            pltpu.VMEM((8, 16, D), BF16),
            pltpu.VMEM((8, 16, D), BF16),
            pltpu.VMEM((3 * D, D), BF16),
            pltpu.VMEM((D, D), BF16),
            pltpu.VMEM((EXT, D), BF16),
            pltpu.VMEM((3 * D, EXT), F32),
            pltpu.VMEM((4, 128, 2 * OWN), BF16),
            pltpu.VMEM((4, 128, EXT), BF16),
            pltpu.VMEM((4, 128, EXT), BF16),
            pltpu.VMEM((4, EXT, 128), BF16),
            pltpu.VMEM((4, EXT, 128), BF16),
            pltpu.VMEM((4, 128, OWN), F32),
            pltpu.VMEM((4, 128, EXT), F32),
            pltpu.VMEM((4, 2, 1, OWN), F32),
            pltpu.VMEM((4, 2, 1, EXT), F32),
            pltpu.VMEM((4, 128, 2 * OWN), BF16),
            pltpu.VMEM((4, 128, OWN), BF16),
            pltpu.VMEM((4, EXT, 2 * OWN), F32),
            pltpu.VMEM((4, EXT, 2 * OWN), BF16),
            pltpu.VMEM((4, 1, 2 * OWN), F32),
            pltpu.VMEM((2, EXT, 2 * OWN), F32),
            pltpu.VMEM((2, EXT, 2 * OWN), BF16),
            pltpu.VMEM((4, 128, OWN), BF16),
            pltpu.VMEM((4, 128, EXT), BF16),
            pltpu.VMEM((4, 128, EXT), BF16),
            pltpu.VMEM((OWN, D), BF16),
            pltpu.VMEM((4, 128, OWN), BF16),
            pltpu.VMEM((EXT, 2 * OWN), F32),
            pltpu.VMEM((4, 2, 128, D), BF16),
            pltpu.VMEM((4, 2, 128, D), BF16),
            pltpu.VMEM((4, 6, 4, 16, 128), BF16),
            pltpu.VMEM((3, 4, 4, 16, 128), BF16),
            pltpu.VMEM((4, 7, 4, 16, 128), BF16),
            pltpu.VMEM((4, 6, 4, 16, 128), BF16),
            pltpu.VMEM((4, 4, 4, 16, 128), BF16),
            pltpu.VMEM((4, 7, 4, 16, 128), BF16),
            pltpu.VMEM((4, 6, 16, 128), BF16),
            pltpu.VMEM((4, 4, 16, 128), BF16),
            pltpu.VMEM((4, 7, 16, 128), BF16),
            pltpu.VMEM((16, 2, 16, 128), BF16),
            pltpu.VMEM((16, 16, 128), BF16),
            pltpu.VMEM((16, 2, 16, 128), BF16),
            pltpu.VMEM((16, 16, D), BF16),
            pltpu.VMEM((16, 16, D), BF16),
            pltpu.VMEM((8, 16, D), BF16),
            pltpu.VMEM((8, 16, D), BF16),
            dma((5,)),
            dma((8,)), dma((8,)),
            dma((1,)), dma((1,)),
            dma((4,)), dma((4,)),
            dma((3,)), dma((3,)),
            dma((1,)), dma((1,)),
            dma((8,)), dma((8,)),
            dma((1,)), dma((1,)),
        ],
        compiler_params=pltpu.CompilerParams(
            collective_id=0, has_side_effects=True, vmem_limit_bytes=57 * 2**20
        ),
    )(slab_tokens, cotangent.reshape(OWN, D), w_qkv, w_out, logit_scale)
    out, gin, gw = pl.pallas_call(
        placed,
        out_shape=(
            jax.ShapeDtypeStruct((OWN, D), BF16),
            jax.ShapeDtypeStruct((2, 16, 4, D), BF16),
            jax.ShapeDtypeStruct((16, D), F32),
        ),
        in_specs=[vmem] * 3,
        out_specs=(vmem,) * 3,
        compiler_params=pltpu.CompilerParams(vmem_limit_bytes=8 * 2**20),
    )(out, gin, gw)
    return out.reshape(2, 2, 32, D), gin, gw


def solution(mesh):
    return jax.shard_map(
        on_device,
        mesh=mesh,
        in_specs=(P("gx", None, "gy", None), P("gx", "gy", None, None), P(), P(), P()),
        out_specs=(P("gx", "gy", None, None), P("gx", None, "gy", None), P(("gx", "gy"), None)),
        check_vma=False,
    )
```

```python
import functools

import jax
import jax.numpy as jnp
from jax import lax
from jax.experimental import pallas as pl
from jax.experimental.pallas import tpu as pltpu
from jax.sharding import PartitionSpec as P

MESH = pl.DeviceIdType.MESH
F32 = jnp.float32
BF16 = jnp.bfloat16

D = 512
HEADS = 8
HEAD_DIM = 64
NX, NY, NZ = 32, 16, 32
GX, GY = 16, 8
OWN = 128
EXT = 384
EPSILON = 1e-06
NEGATIVE = -1e30
FACTOR = 1.0 / 128.0

SIDES = ((-1, 0), (1, 0), (0, -1), (0, 1), (-1, -1), (-1, 1), (1, -1), (1, 1))
REGION = {
    (-1, 0): (8, 4),
    (1, 0): (12, 4),
    (0, -1): (16, 2),
    (0, 1): (18, 2),
    (-1, -1): (20, 1),
    (-1, 1): (21, 1),
    (1, -1): (22, 1),
    (1, 1): (23, 1),
}


def dot_nn(a, b):
    return jnp.dot(a, b, preferred_element_type=F32)


def dot_nt(a, b):
    return lax.dot_general(a, b, (((1,), (1,)), ((), ())), preferred_element_type=F32)


def dot_tn(a, b):
    return lax.dot_general(a, b, (((0,), (0,)), ((), ())), preferred_element_type=F32)


def iota(shape, dim):
    return lax.broadcasted_iota(jnp.int32, shape, dim)


def natural_row(r):
    return ((r >> 3) & 1) * 64 + (r & 1) * 32 + (r >> 4) * 4 + ((r >> 1) & 3)


def token_row(r):
    return ((r >> 3) & 1) * 64 + ((r >> 1) & 3) * 16 + (r >> 4) * 2 + (r & 1)


def slab_row(t):
    return ((t >> 6) & 1) * 64 + (t & 15) * 4 + ((t >> 4) & 3)


def gather_rows(index):
    shape = (OWN, OWN)
    return jnp.where(index(iota(shape, 0)) == iota(shape, 1), 1.0, 0.0).astype(BF16)


def scatter_rows(index):
    shape = (OWN, OWN)
    return jnp.where(index(iota(shape, 1)) == iota(shape, 0), 1.0, 0.0).astype(BF16)


def moved(matrix, rows):
    return dot_nn(matrix, rows).astype(BF16)


SLOT_X = {(0, 1): 0, (0, 3): 1, (1, 1): 2, (2, 1): 3, (3, 0): 4, (3, 1): 5}
SLOT_Z = {(0, 2): 0, (1, 2): 1, (1, 3): 2, (2, 2): 3, (2, 3): 4, (3, 2): 5, (3, 3): 6}
SPAN_X = ((0, 2), (2, 1), (3, 1), (4, 2))
SPAN_Z = ((0, 1), (1, 2), (3, 2), (5, 2))


def kernel(
    slab_hbm, cot_hbm, wqkv_hbm, wout_hbm, scale_hbm,
    out, gin, gw,
    slab, xs, cot, scale, xext, cot_send, cot_stage, wqkv, wout, normed, raw,
    q_bd, k_b, v_b, k_t, v_t, q_hat, k_hat, q_inv, k_inv, u_bd, att,
    weights_f, weights_b, inverse, grad_f, grad_b, gq, gk, gv, cot_tok, cot_t, bias,
    pair_send, pair_recv, sx, sy, sz, rx, ry, rz, tx, ty, tz, fx, fy, fz,
    gn_send, gn_recv, out_send, out_stage,
    w_sem, x_ssem, x_rsem, c_ssem, c_rsem, p_ssem, p_rsem,
    a_ssem, a_rsem, b_ssem, b_rsem, g_ssem, g_rsem, o_ssem, o_rsem,
):
    gx, gy = lax.axis_index("gx"), lax.axis_index("gy")
    core = gx & 1
    at_y = gx >> 2
    at_x = ((gx >> 1) & 1) * 2 + (gy & 1)
    at_z = gy >> 1

    def device_at(y, x, z):
        return (y * 4 + (x >> 1) * 2 + core, z * 2 + (x & 1))

    def exists(side):
        ok = None
        for at, step, size in ((gx, side[0], GX), (gy, side[1], GY)):
            if step:
                here = at > 0 if step < 0 else at < size - 1
                ok = here if ok is None else ok & here
        return ok

    def remote(src, dst, ssem, rsem, to):
        return pltpu.make_async_remote_copy(
            src_ref=src, dst_ref=dst, send_sem=ssem, recv_sem=rsem,
            device_id=to, device_id_type=MESH,
        )

    def wait_for(ref, sem):
        pltpu.make_async_copy(ref, ref, sem).wait()

    load_cot = pltpu.make_async_copy(cot_hbm, cot, w_sem.at[0])
    load_slab = pltpu.make_async_copy(slab_hbm, slab, w_sem.at[1])
    load_scale = pltpu.make_async_copy(scale_hbm, scale, w_sem.at[2])
    load_qkv = pltpu.make_async_copy(wqkv_hbm, wqkv, w_sem.at[3])
    load_out = pltpu.make_async_copy(wout_hbm, wout, w_sem.at[4])
    load_slab.start()
    load_cot.start()
    load_scale.start()
    load_qkv.start()
    load_out.start()

    barrier = pltpu.get_barrier_semaphore()

    def greet(to):
        pl.semaphore_signal(barrier, inc=1, device_id=to, device_id_type=MESH)

    for side in SIDES:
        if side[0]:
            @pl.when(exists(side))
            def _():
                greet((gx + side[0], gy + side[1]))

    def greet_plane(k, carry):
        x, z = (at_x + (k >> 2)) & 3, (at_z + k) & 3
        greet(device_at(at_y, x, z))
        return carry

    def greet_lines(k, carry):
        y = (at_y + 1 + (k >> 2)) & 3
        greet(device_at(y, at_x, (at_z + k) & 3))

        @pl.when((k & 3) > 0)
        def _():
            greet(device_at(y, (at_x + k) & 3, at_z))

        return carry

    lax.fori_loop(1, 16, greet_plane, 0, unroll=15)
    lax.fori_loop(0, 12, greet_lines, 0, unroll=12)

    load_slab.wait()
    slab_rows = slab[...].astype(F32).reshape(OWN, D).astype(BF16)
    xs[...] = moved(gather_rows(slab_row), slab_rows).reshape(2, 4, 16, D)
    one = jnp.int32(1)
    zero = jnp.int32(0)
    count_x = jnp.where(gx > 0, one, zero) + jnp.where(gx < GX - 1, one, zero)
    count_y = one + jnp.where(gy > 0, one, zero) + jnp.where(gy < GY - 1, one, zero)
    pl.semaphore_wait(barrier, 36 + count_x * count_y)

    def border(ref, side):
        x = {-1: 0, 1: 1}.get(side[0])
        z = {-1: 0, 1: 3}.get(side[1])
        if z is None:
            return ref.at[x]
        if x is None:
            return ref.at[:, z]
        return ref.at[pl.ds(x, 1), z]

    def halo_copy(index, side):
        start, size = REGION[(-side[0], -side[1])]
        return remote(
            border(xs, side), xext.at[pl.ds(start, size)],
            x_ssem.at[index], x_rsem.at[index], (gx + side[0], gy + side[1]),
        )

    for index, side in enumerate(SIDES):
        @pl.when(exists(side))
        def _():
            halo_copy(index, side).start()

    load_cot.wait()
    cot_send[...] = moved(gather_rows(natural_row), cot[...]).reshape(8, 16, D)
    load_scale.wait()

    def cot_copy(k, carry):
        to = (gy + k) & (GY - 1)
        remote(
            cot_send.at[to], cot_stage.at[gy], c_ssem.at[0], c_rsem.at[0], (gx, to)
        ).start()
        return carry

    for side in SIDES:
        start, size = REGION[side]

        @pl.when(jnp.logical_not(exists(side)))
        def _():
            xext[pl.ds(start, size)] = jnp.zeros((size, 16, D), BF16)
            gn_recv[pl.ds(start - 8, size)] = jnp.zeros((size, 16, D), BF16)

    def rows_normed(rows):
        return rows * lax.rsqrt(jnp.mean(rows * rows, axis=-1, keepdims=True) + EPSILON)

    x_rows = xs[...].reshape(OWN, D)
    normed[0:OWN] = rows_normed(x_rows.astype(F32)).astype(BF16)
    load_qkv.wait()
    raw[:, 0:OWN] = dot_nt(wqkv[...], normed[0:OWN])

    def pair_rows(base, j):
        return pl.ds(pl.multiple_of(base + j * 128, 128), 128)

    def heads_of(values):
        return values.reshape(2, HEAD_DIM, values.shape[1])

    def head_inverse(values):
        return lax.rsqrt(jnp.mean(values * values, axis=1, keepdims=True) + EPSILON)

    q_bd[...] = jnp.zeros_like(q_bd)
    u_bd[...] = jnp.zeros_like(u_bd)

    def keys_values(j, low, high):
        k = heads_of(raw[pair_rows(D, j), low:high])
        rms = head_inverse(k)
        hat = (k * rms).reshape(128, high - low)
        k_hat[j, :, low:high] = hat
        k_inv[j, :, :, low:high] = rms
        hat_b = hat.astype(BF16)
        k_b[j, :, low:high] = hat_b
        k_t[j, low:high] = hat_b.T
        v = raw[pair_rows(2 * D, j), low:high].astype(BF16)
        v_b[j, :, low:high] = v
        v_t[j, low:high] = v.T

    def own_pairs(j, carry):
        q = heads_of(raw[pair_rows(0, j), 0:OWN])
        rms = head_inverse(q)
        hat = q * rms
        q_hat[j] = hat.reshape(128, OWN)
        q_inv[j] = rms
        for s in range(2):
            q_bd[j, 64 * s : 64 * s + 64, 128 * s : 128 * s + 128] = (
                hat[s] * (scale[2 * j + s] / HEAD_DIM)
            ).astype(BF16)
        keys_values(j, 0, OWN)
        return carry

    lax.fori_loop(0, 4, own_pairs, 0)

    col = iota((16, OWN), 1)
    row_y = iota((16, OWN), 0)
    col_x, col_z = col >> 6, (col >> 4) & 3
    near_y = jnp.abs(row_y - (col & 15)) <= 1

    def bias_cell(cell, carry):
        x = jnp.where(
            cell < 8,
            cell >> 2,
            jnp.where(
                cell < 16,
                jnp.where(cell < 12, -1, 2),
                jnp.where(cell < 20, cell & 1, jnp.where(cell < 22, -1, 2)),
            ),
        )
        z = jnp.where(
            cell < 16,
            cell & 3,
            jnp.where(
                cell < 20, jnp.where(cell < 18, -1, 4), jnp.where((cell & 1) == 0, -1, 4)
            ),
        )
        full_x, full_z = x + 2 * gx, z + 4 * gy
        inside = (full_x >= 0) & (full_x < NX) & (full_z >= 0) & (full_z < NZ)
        x_off = jnp.where(inside, x, jnp.int32(100))
        near = near_y & (jnp.abs(x_off - col_x) <= 1) & (jnp.abs(z - col_z) <= 1)
        block = jnp.where(near, 0.0, NEGATIVE)
        rows = pl.ds(pl.multiple_of(cell * 16, 16), 16)
        bias[rows, 0:OWN] = block
        bias[rows, OWN : 2 * OWN] = block
        return carry

    lax.fori_loop(0, 24, bias_cell, 0)

    lax.fori_loop(1, GY, cot_copy, 0)
    cot_stage[gy] = cot_send[gy]

    for index, side in enumerate(SIDES):
        opposite = SIDES.index((-side[0], -side[1]))
        start, size = REGION[side]

        @pl.when(exists(side))
        def _():
            wait_for(xext.at[pl.ds(start, size)], x_rsem.at[opposite])

    halo_rows = xext[8:24].reshape(EXT - OWN, D)
    normed[OWN:EXT] = rows_normed(halo_rows.astype(F32)).astype(BF16)
    raw[D : 3 * D, OWN:EXT] = dot_nt(wqkv[D : 3 * D], normed[OWN:EXT])

    def halo_pairs(j, carry):
        keys_values(j, OWN, EXT)
        return carry

    lax.fori_loop(0, 4, halo_pairs, 0, unroll=4)

    steps = [slice(low, low + 128) for low in range(0, EXT, 128)]
    halves = [(slice(64 * s, 64 * s + 64), slice(128 * s, 128 * s + 128)) for s in range(2)]

    def score_step(j, rows, top):
        scores = dot_nn(k_t[j, rows], q_bd[j]) + bias[rows]
        weights_f[j, rows] = scores
        here = jnp.max(scores, axis=0, keepdims=True)
        return here if top is None else jnp.maximum(top, here)

    def exp_step(j, rows, top, total):
        shifted = jnp.exp(weights_f[j, rows] - top)
        weights_f[j, rows] = shifted
        weights_b[j, rows] = shifted.astype(BF16)
        here = jnp.sum(shifted, axis=0, keepdims=True)
        return here if total is None else total + here

    def attend(j, total):
        scaled = 1.0 / total
        inverse[j] = scaled
        for rows, cols in halves:
            att[j, rows] = (
                dot_nn(v_b[j, rows], weights_b[j, :, cols]) * scaled[:, cols]
            ).astype(BF16)

    def forward_pairs():
        tops = [None] * 5
        for j in range(5):
            total = None
            for rows in steps:
                if j < 4:
                    tops[j] = score_step(j, rows, tops[j])
                if j:
                    total = exp_step(j - 1, rows, tops[j - 1], total)
            if j:
                attend(j - 1, total)

    def back_through(grad, hat, inverse_rms):
        return inverse_rms * (grad - hat * jnp.mean(grad * hat, axis=0, keepdims=True))

    def grad_weight_step(j, t, rows, inner):
        grad_w = dot_nn(v_t[j, rows], u_bd[j])
        grad_f[t, rows] = grad_w
        here = jnp.sum(weights_f[j, rows] * grad_w, axis=0, keepdims=True)
        return here if inner is None else inner + here

    def grad_score_step(j, t, rows, inner):
        scaled = inverse[j]
        grad_b[t, rows] = (
            weights_f[j, rows] * ((grad_f[t, rows] - inner * scaled) * scaled)
        ).astype(BF16)

    def grad_heads(j, t, s):
        rows, cols = halves[s]
        grad_q = dot_nn(k_b[j, rows], grad_b[t, :, cols])
        gq[j, rows] = (
            back_through(grad_q, q_hat[j, rows], q_inv[j, s]) * (scale[2 * j + s] / HEAD_DIM)
        ).astype(BF16)
        grad_k = dot_nt(q_bd[j, rows, cols], grad_b[t, :, cols])
        gk[j, rows] = back_through(grad_k, k_hat[j, rows], k_inv[j, s]).astype(BF16)
        up = (u_bd[j, rows, cols].astype(F32) * inverse[j][:, cols]).astype(BF16)
        gv[j, rows] = dot_nt(up, weights_b[j, :, cols]).astype(BF16)

    def backward_pairs(first, second):
        inner = [None, None]
        for rows in steps:
            inner[0] = grad_weight_step(first, 0, rows, inner[0])
        for rows in steps:
            inner[1] = grad_weight_step(second, 1, rows, inner[1])
            grad_score_step(first, 0, rows, inner[0])
        grad_heads(first, 0, 0)
        for rows in steps:
            grad_score_step(second, 1, rows, inner[1])
        grad_heads(first, 0, 1)
        for s in range(2):
            grad_heads(second, 1, s)

    def weight_block(part, j):
        if part == 3:
            return dot_nt(cot_t[j], att[...].reshape(D, OWN))
        if part == 0:
            return dot_nn(gq[j], normed[0:OWN])
        return dot_nn((gk if part == 1 else gv)[j], normed[...])

    def pair_copy(part):
        return remote(
            pair_send.at[part], pair_recv.at[part],
            p_ssem.at[part], p_rsem.at[part], (gx + 1 - 2 * core, gy),
        )

    def send_other(part):
        for which in range(2):
            block = weight_block(part, 2 * which + 1 - core)
            pair_send[part, which] = block.astype(BF16)
        pair_copy(part).start()

    def sum_own(part):
        pair_copy(part).wait_recv()
        for which in range(2):
            total = weight_block(part, 2 * which + core) + pair_recv[part, which].astype(F32)
            blocks = total.astype(BF16).reshape(8, 16, D)
            for r in range(8):
                x, z = 2 * which + (r & 1), r >> 1
                for tile in range(4):
                    value = blocks[r, :, 128 * tile : 128 * tile + 128]
                    if (part, tile) in SLOT_X:
                        sx[x, SLOT_X[part, tile], z] = value
                    elif (part, tile) in SLOT_Z:
                        sz[z, SLOT_Z[part, tile], x] = value
                    else:
                        sy[part, x, z] = value

    def send_lines(slots_x, slots_z):
        def step(k, carry):
            z = (at_z + k) & 3
            remote(
                sz.at[z, slots_z], rz.at[at_z, slots_z], a_ssem.at[2], a_rsem.at[2],
                device_at(at_y, at_x, z),
            ).start()
            x = (at_x + k) & 3
            remote(
                sx.at[x, slots_x], rx.at[at_x, slots_x], a_ssem.at[0], a_rsem.at[0],
                device_at(at_y, x, at_z),
            ).start()
            return carry

        for k in range(1, 4):
            step(k, 0)

    def send_y(part):
        @pl.when(at_y != part)
        def _():
            remote(
                sy.at[part], ry.at[at_y], a_ssem.at[1], a_rsem.at[1],
                device_at(part, at_x, at_z),
            ).start()

    forward_pairs()

    load_out.wait()
    wait_for(cot_stage.at[pl.ds(0, GY - 1)], c_rsem.at[0])
    tokens = moved(scatter_rows(token_row), cot_stage[...].reshape(OWN, D))
    cot_tok[...] = tokens
    cot_t[...] = tokens.T.reshape(4, 128, OWN)
    upstream = dot_nn(tokens, wout[...]).astype(BF16).T
    for j in range(4):
        for s in range(2):
            u_bd[j, 64 * s : 64 * s + 64, 128 * s : 128 * s + 128] = upstream[
                128 * j + 64 * s : 128 * j + 64 * s + 64
            ]

    send_other(3)
    attended = att[...].reshape(D, OWN).T
    out_rows = (x_rows.astype(F32) + dot_nt(attended, wout[...])).astype(BF16)
    out_send[...] = moved(gather_rows(token_row), out_rows).reshape(8, 16, D)

    def out_copy(k, carry):
        to = (gy + k) & (GY - 1)
        remote(
            out_send.at[to], out_stage.at[gy], o_ssem.at[0], o_rsem.at[0], (gx, to)
        ).start()
        return carry

    lax.fori_loop(1, GY, out_copy, 0)
    out_stage[gy] = out_send[gy]

    backward_pairs(1 - core, 3 - core)
    for part in range(3):
        send_other(part)
    sum_own(3)
    send_lines(pl.ds(4, 2), pl.ds(5, 2))
    backward_pairs(core, 2 + core)
    for part in (0, 2, 1):
        sum_own(part)
        send_y(part)
        send_lines(pl.ds(*SPAN_X[part]), pl.ds(*SPAN_Z[part]))

    grad_kv_halo = jnp.concatenate(
        [gk[:, :, OWN:EXT].reshape(D, EXT - OWN), gv[:, :, OWN:EXT].reshape(D, EXT - OWN)],
        axis=0,
    )
    gn_send[...] = (
        dot_tn(grad_kv_halo, wqkv[D : 3 * D]).astype(BF16).reshape(16, 16, D)
    )

    def grad_copy(index, side):
        start, size = REGION[side]
        target, _ = REGION[(-side[0], -side[1])]
        return remote(
            gn_send.at[pl.ds(start - 8, size)], gn_recv.at[pl.ds(target - 8, size)],
            g_ssem.at[index], g_rsem.at[index], (gx + side[0], gy + side[1]),
        )

    for index, side in enumerate(SIDES):
        @pl.when(exists(side))
        def _():
            grad_copy(index, side).start()

    wait_for(out_stage.at[pl.ds(0, GY - 1)], o_rsem.at[0])
    out[...] = moved(scatter_rows(natural_row), out_stage[...].reshape(OWN, D))

    grad_own = jnp.concatenate(
        [
            gq[...].reshape(D, OWN),
            gk[:, :, 0:OWN].reshape(D, OWN),
            gv[:, :, 0:OWN].reshape(D, OWN),
        ],
        axis=0,
    )
    grad_n = dot_tn(grad_own, wqkv[...]).reshape(2, 4, 16, D)
    def line_sum(own, others, me):
        ry_ = own.astype(F32)
        for k in range(1, 4):
            ry_ = ry_ + others[(me + k) & 3].astype(F32)
        return ry_.astype(BF16)

    @pl.when(at_y < 3)
    def _():
        wait_for(ry.at[pl.ds(0, 3)], a_rsem.at[1])
        ty[...] = line_sum(sy[at_y], ry, at_y)

        def send_ty(k, carry):
            x, z = (at_x + (k >> 2)) & 3, (at_z + k) & 3
            remote(
                ty.at[x, z], fy.at[at_x * 4 + at_z], b_ssem.at[0], b_rsem.at[0],
                device_at(at_y, x, z),
            ).start()
            return carry

        lax.fori_loop(1, 16, send_ty, 0, unroll=5)
        fy[at_x * 4 + at_z] = ty[at_x, at_z]

    def second_step(line, own, others, me, sums, spans, landing, sem, target):
        wait_for(others.at[pl.ds(0, 3)], sem)
        total = line_sum(own[me], others, me)
        for slot in range(total.shape[0]):
            for at in range(4):
                sums[at, slot] = total[slot, at]
        for y in range(4):
            first, count = spans[y]

            def send(k, carry):
                to = (line + k) & 3
                remote(
                    sums.at[to, pl.ds(first, count)],
                    landing.at[at_y * 4 + line, pl.ds(0, count)],
                    b_ssem.at[0], b_rsem.at[0], target(y, to),
                ).start()
                return carry

            for k in range(1, 4):
                send(k, 0)

            @pl.when(at_y != y)
            def _():
                send(0, 0)

            @pl.when(at_y == y)
            def _():
                landing[at_y * 4 + line, 0:count] = sums[line, first : first + count]

    second_step(
        at_z, sx, rx, at_x, tx, SPAN_X, fx, a_rsem.at[0], lambda y, z: device_at(y, at_x, z)
    )
    second_step(
        at_x, sz, rz, at_z, tz, SPAN_Z, fz, a_rsem.at[2], lambda y, x: device_at(y, x, at_z)
    )

    for index, side in enumerate(SIDES):
        opposite = SIDES.index((-side[0], -side[1]))
        start, size = REGION[side]

        @pl.when(exists(side))
        def _():
            wait_for(gn_recv.at[pl.ds(start - 8, size)], g_rsem.at[opposite])

    def term(side):
        start, size = REGION[side]
        return gn_recv[start - 8 : start - 8 + size].astype(F32)

    planes = []
    for x in range(2):
        side_x = (-1, 1)[x]
        plane = grad_n[x] + term((side_x, 0))
        low = term((0, -1))[x] + term((side_x, -1))[0]
        high = term((0, 1))[x] + term((side_x, 1))[0]
        planes.append(
            jnp.concatenate(
                [plane[0:1] + low[None], plane[1:3], plane[3:4] + high[None]], axis=0
            )
        )
    grad_n = jnp.concatenate(planes, axis=0).reshape(OWN, D)
    x_float = x_rows.astype(F32)
    x_inv = lax.rsqrt(jnp.mean(x_float * x_float, axis=-1, keepdims=True) + EPSILON)
    x_hat = x_float * x_inv
    grad_x = x_inv * (grad_n - x_hat * jnp.mean(grad_n * x_hat, axis=-1, keepdims=True))
    grad_rows = (cot_tok[...].astype(F32) + grad_x).astype(BF16)
    gin[...] = moved(scatter_rows(slab_row), grad_rows)

    wait_for(rz.at[pl.ds(0, 3), pl.ds(0, 5)], b_rsem.at[0])

    def put(tile, blocks):
        gw[:, 128 * tile : 128 * tile + 128] = jnp.sum(blocks.astype(F32), axis=0) * FACTOR

    @pl.when(at_y < 3)
    def _():
        put(0, fy[...])
        put(1, fx[:, 0])

    @pl.when(at_y == 3)
    def _():
        put(0, fx[:, 0])
        put(1, fx[:, 1])

    put(2, fz[:, 0])

    @pl.when(at_y == 0)
    def _():
        put(3, fx[:, 1])

    @pl.when(at_y > 0)
    def _():
        put(3, fz[:, 1])

    for index, side in enumerate(SIDES):
        @pl.when(exists(side))
        def _():
            halo_copy(index, side).wait_send()
            grad_copy(index, side).wait_send()

    for part in range(4):
        pair_copy(part).wait_send()
    wait_for(cot_send.at[pl.ds(0, GY - 1)], c_ssem.at[0])
    wait_for(out_send.at[pl.ds(0, GY - 1)], o_ssem.at[0])
    wait_for(rx.at[pl.ds(0, 3)], a_ssem.at[0])
    wait_for(rz.at[pl.ds(0, 3)], a_ssem.at[2])

    @pl.when(at_y < 3)
    def _():
        wait_for(ry.at[pl.ds(0, 2)], a_ssem.at[1])
        wait_for(rz.at[pl.ds(0, 4), pl.ds(0, 4)], b_ssem.at[0])

    @pl.when(at_y == 3)
    def _():
        wait_for(ry.at[pl.ds(0, 3)], a_ssem.at[1])
        wait_for(rz.at[pl.ds(0, 3), pl.ds(0, 4)], b_ssem.at[0])


def placed(out, gin, gw, out_at, gin_at, gw_at):
    out_at[...] = out[...]
    gin_at[...] = gin[...].astype(F32).reshape(2, 16, 4, D).astype(BF16)
    gw_at[...] = gw[...]


def on_device(slab_tokens, cotangent, w_qkv, w_out, logit_scale):
    vmem = pl.BlockSpec(memory_space=pltpu.VMEM)
    hbm = pl.BlockSpec(memory_space=pl.ANY)
    dma = pltpu.SemaphoreType.DMA
    out, gin, gw = pl.pallas_call(
        kernel,
        out_shape=(
            pltpu.VMEM((OWN, D), BF16),
            pltpu.VMEM((OWN, D), BF16),
            pltpu.VMEM((16, D), F32),
        ),
        in_specs=[hbm] * 5,
        out_specs=(vmem, vmem, vmem),
        scratch_shapes=[
            pltpu.VMEM((2, 16, 4, D), BF16),
            pltpu.VMEM((2, 4, 16, D), BF16),
            pltpu.VMEM((OWN, D), BF16),
            pltpu.SMEM((HEADS,), F32),
            pltpu.VMEM((24, 16, D), BF16),
            pltpu.VMEM((8, 16, D), BF16),
            pltpu.VMEM((8, 16, D), BF16),
            pltpu.VMEM((3 * D, D), BF16),
            pltpu.VMEM((D, D), BF16),
            pltpu.VMEM((EXT, D), BF16),
            pltpu.VMEM((3 * D, EXT), F32),
            pltpu.VMEM((4, 128, 2 * OWN), BF16),
            pltpu.VMEM((4, 128, EXT), BF16),
            pltpu.VMEM((4, 128, EXT), BF16),
            pltpu.VMEM((4, EXT, 128), BF16),
            pltpu.VMEM((4, EXT, 128), BF16),
            pltpu.VMEM((4, 128, OWN), F32),
            pltpu.VMEM((4, 128, EXT), F32),
            pltpu.VMEM((4, 2, 1, OWN), F32),
            pltpu.VMEM((4, 2, 1, EXT), F32),
            pltpu.VMEM((4, 128, 2 * OWN), BF16),
            pltpu.VMEM((4, 128, OWN), BF16),
            pltpu.VMEM((4, EXT, 2 * OWN), F32),
            pltpu.VMEM((4, EXT, 2 * OWN), BF16),
            pltpu.VMEM((4, 1, 2 * OWN), F32),
            pltpu.VMEM((2, EXT, 2 * OWN), F32),
            pltpu.VMEM((2, EXT, 2 * OWN), BF16),
            pltpu.VMEM((4, 128, OWN), BF16),
            pltpu.VMEM((4, 128, EXT), BF16),
            pltpu.VMEM((4, 128, EXT), BF16),
            pltpu.VMEM((OWN, D), BF16),
            pltpu.VMEM((4, 128, OWN), BF16),
            pltpu.VMEM((EXT, 2 * OWN), F32),
            pltpu.VMEM((4, 2, 128, D), BF16),
            pltpu.VMEM((4, 2, 128, D), BF16),
            pltpu.VMEM((4, 6, 4, 16, 128), BF16),
            pltpu.VMEM((3, 4, 4, 16, 128), BF16),
            pltpu.VMEM((4, 7, 4, 16, 128), BF16),
            pltpu.VMEM((4, 6, 4, 16, 128), BF16),
            pltpu.VMEM((4, 4, 4, 16, 128), BF16),
            pltpu.VMEM((4, 7, 4, 16, 128), BF16),
            pltpu.VMEM((4, 6, 16, 128), BF16),
            pltpu.VMEM((4, 4, 16, 128), BF16),
            pltpu.VMEM((4, 7, 16, 128), BF16),
            pltpu.VMEM((16, 2, 16, 128), BF16),
            pltpu.VMEM((16, 16, 128), BF16),
            pltpu.VMEM((16, 2, 16, 128), BF16),
            pltpu.VMEM((16, 16, D), BF16),
            pltpu.VMEM((16, 16, D), BF16),
            pltpu.VMEM((8, 16, D), BF16),
            pltpu.VMEM((8, 16, D), BF16),
            dma((5,)),
            dma((8,)), dma((8,)),
            dma((1,)), dma((1,)),
            dma((4,)), dma((4,)),
            dma((3,)), dma((3,)),
            dma((1,)), dma((1,)),
            dma((8,)), dma((8,)),
            dma((1,)), dma((1,)),
        ],
        compiler_params=pltpu.CompilerParams(
            collective_id=0, has_side_effects=True, vmem_limit_bytes=57 * 2**20
        ),
    )(slab_tokens, cotangent.reshape(OWN, D), w_qkv, w_out, logit_scale)
    out, gin, gw = pl.pallas_call(
        placed,
        out_shape=(
            jax.ShapeDtypeStruct((OWN, D), BF16),
            jax.ShapeDtypeStruct((2, 16, 4, D), BF16),
            jax.ShapeDtypeStruct((16, D), F32),
        ),
        in_specs=[vmem] * 3,
        out_specs=(vmem,) * 3,
        compiler_params=pltpu.CompilerParams(vmem_limit_bytes=8 * 2**20),
    )(out, gin, gw)
    return out.reshape(2, 2, 32, D), gin, gw


def solution(mesh):
    return jax.shard_map(
        on_device,
        mesh=mesh,
        in_specs=(P("gx", None, "gy", None), P("gx", "gy", None, None), P(), P(), P()),
        out_specs=(P("gx", "gy", None, None), P("gx", None, "gy", None), P(("gx", "gy"), None)),
        check_vma=False,
    )
```
